512 devices in a mesh: space: 128 (over x, z_hi, y), lag: 4 (over z_lo, core).
Axes of the slice: x: 4, y: 8, z: 8 (z_hi: 4, z_lo: 2; z = z_hi * 2 + z_lo), core: 2. Of those that a mesh axis runs over, the one named last changes fastest.
Arguments:
- ensemble: bfloat16 [4, 2048, 64, 512], P('lag', 'space'), may hold values from -6 to 6
- obs_anomaly: float32 [64, 1048576], P(None, ('space', 'lag')), may hold values from -1 to 1
- innovation: float32 [1048576], P(('space', 'lag')), may hold values from -6 to 6
- inv_variance: float32 [1048576], P(('space', 'lag')), may hold values from 0.1 to 1
- obs_column: int32 [1048576], P(('space', 'lag')), may hold values from 0 to 15
- obs_count: int32 [512], P(('space', 'lag')), may hold values from 256 to 2048
- taper: float32 [32], replicated, may hold values from 0.1 to 1
Outputs:
- analysis: bfloat16 [4, 2048, 64, 512], P('lag', 'space')
The draws below stay inside these ranges and needn't reach their ends.
All inputs are finite; a program needn't handle non-finite values.
Results may differ from the reference program's by a relative error of at most 0.0075.
Values may be sent and summed in bfloat16 or wider, within the bound.
No kernel may reach another device: no remote copies, remote signals or barrier semaphores. Data moves between devices by JAX's collectives and lax.ppermute only.
A program may use at most 64 MiB of HBM per device.

```python
import math
import jax
import jax.numpy as jnp
from jax import lax

K = 64
CC = 16
PTS = 512
OBS_L = 2048
NS_ITERS = 4
COLS = 2048
OBS_SHARDS = 512
OBS_ALL = 1048576
REACH = 32
N_SPACE = 128
N_LAG = 4


def draw_obs_count(key, part):
    first = jax.random.fold_in(key, 11)
    second = jax.random.fold_in(key, 12)
    counts = jax.random.randint(first, (OBS_SHARDS,), OBS_L // 8, OBS_L + 1).astype(jnp.int32)
    where = jax.random.randint(second, (), 0, OBS_SHARDS)
    return counts.at[where].set(OBS_L).astype(jnp.int32)


def place_ends(values, own_key, least, top_value):
    place = [jax.random.randint(jax.random.fold_in(own_key, axis), (), 0, length) for axis, length in enumerate(values.shape)]
    main_axis = values.shape.index(max(values.shape))
    beside = place[:main_axis] + [(place[main_axis] + 1) % values.shape[main_axis]] + place[main_axis + 1:]
    return values.at[tuple(place)].set(least).at[tuple(beside)].set(top_value)


def block_scale(key, shape, cuts, low, largest):
    factor_of = 1.0
    for position, blocks in cuts:
        draws = jax.random.uniform(jax.random.fold_in(jax.random.fold_in(key, 6), position), (blocks,), jnp.float32, low / len(cuts), largest / len(cuts))
        factor_of = factor_of * jnp.repeat(jnp.exp(draws), shape[position] // blocks).reshape((-1,) + (1,) * (len(shape) - 1 - position))
    return factor_of


def bell_draw(own_key, extent, spread, most, shards=(), kind=jnp.bfloat16):
    values = spread * jax.random.normal(own_key, extent, jnp.float32)
    if shards:
        values = values * block_scale(own_key, extent, shards, -0.22, 0.18)
    return jnp.clip(values, -most, most).astype(kind)


def setup_inputs(seed: int = 0) -> dict:
    streams_of = jax.random.split(jax.random.key(seed), 8)
    return {
        "ensemble": bell_draw(streams_of[0], (N_LAG, COLS, K, PTS), 1.0, 6.0, ((0, 4), (1, 128))),
        "obs_anomaly": bell_draw(streams_of[1], (K, OBS_ALL), 0.15, 1.0, ((1, 512),), jnp.float32),
        "innovation": bell_draw(streams_of[2], (OBS_ALL,), 1.0, 6.0, ((0, 512),), jnp.float32),
        "inv_variance": jnp.clip(jnp.exp(math.log(1.0) - 2.3025851 * jax.random.uniform(streams_of[3], (OBS_ALL,), jnp.float32) ** block_scale(streams_of[3], (OBS_ALL,), ((0, 512),), -0.2, 0.2)), 0.1, 1.0),
        "obs_column": place_ends(jax.random.randint(streams_of[4], (OBS_ALL,), 0, CC), jax.random.fold_in(streams_of[4], 1), 0, CC - 1).astype(jnp.int32),
        "obs_count": draw_obs_count(jax.random.fold_in(streams_of[7], 71), 0),
        "taper": jnp.clip(jnp.exp(jax.random.uniform(streams_of[6], (REACH,), jnp.float32, math.log(0.1), math.log(1.0))), 0.1, 1.0),
    }


HIGH = lax.Precision.HIGHEST

def column_weights(positions, rinv, taper, ncol):
    reach = taper.shape[0]
    targets = jnp.arange(ncol, dtype=jnp.int32)
    slots = jnp.arange(3 * ncol, dtype=jnp.int32) - ncol
    dist = jnp.abs(targets[:, None] - slots[None, :])
    pick = (dist[:, :, None] == jnp.arange(reach, dtype=jnp.int32)[None, None, :]).astype(jnp.float32)
    table = jnp.dot(pick, taper, precision=HIGH)
    onehot = (positions[:, None] + ncol == jnp.arange(3 * ncol, dtype=jnp.int32)[None, :]).astype(jnp.float32)
    return jnp.dot(table, onehot.T, precision=HIGH) * rinv[None, :]

def gram_of(extended, weights):
    anomal = extended[:-1]

    def single(wcol):
        return jnp.dot(extended * wcol[None, :], anomal.T, precision=HIGH)
    return lax.map(single, weights)

def transform(gram, members):
    eye = jnp.eye(members, dtype=jnp.float32)
    amat = gram[:, :members, :] + (members - 1.0) * eye
    bvec = gram[:, members, :]
    scale = jnp.sqrt(lax.optimization_barrier(jnp.sum(amat * amat, axis=(1, 2))))
    yval = amat / scale[:, None, None]
    zval = jnp.broadcast_to(eye, amat.shape)
    for step in range(NS_ITERS):
        mval = 1.5 * eye - 0.5 * jnp.einsum('cij,cjk->cik', zval, yval, precision=HIGH)
        yval = jnp.einsum('cij,cjk->cik', yval, mval, precision=HIGH)
        zval = jnp.einsum('cij,cjk->cik', mval, zval, precision=HIGH)
    inner = jnp.einsum('cij,cj->ci', zval, bvec, precision=HIGH)
    shift = jnp.einsum('cij,cj->ci', zval, inner, precision=HIGH) / scale[:, None]
    result = jnp.sqrt(members - 1.0) * zval / jnp.sqrt(scale)[:, None, None] + shift[:, :, None]
    return result.astype(jnp.bfloat16)

def apply_weights(weights, block):
    members = block.astype(jnp.float32)
    mean = lax.optimization_barrier(jnp.mean(members, axis=2))
    anomalies = (members - mean[:, :, None, :]).astype(jnp.bfloat16)
    mixed = jnp.einsum('ckj,lckp->lcjp', weights.astype(jnp.float32), anomalies.astype(jnp.float32))
    return (mean[:, :, None, :] + mixed).astype(jnp.bfloat16)

def reference(ensemble, obs_anomaly, innovation, inv_variance, obs_column, obs_count, taper):
    tiles = N_SPACE
    per = N_LAG * OBS_L
    anom = obs_anomaly.reshape(K, tiles, per)
    innov = innovation.reshape(tiles, per)
    cols = obs_column.reshape(tiles, per)
    counts = obs_count.reshape(tiles, N_LAG)
    slot = jnp.arange(per, dtype=jnp.int32)
    owner = slot // OBS_L
    live = slot[None, :] % OBS_L < counts[:, owner]
    rinv_all = inv_variance.reshape(tiles, per) * live.astype(jnp.float32)
    ens = ensemble.reshape(N_LAG, tiles, CC, K, PTS)

    def tile(index):
        parts = []
        poss = []
        rinvs = []
        for side in range(3):
            other = (index + side - 1 + tiles) % tiles
            parts.append(jnp.concatenate([anom[:, other], innov[other][None, :]], axis=0))
            poss.append(cols[other] + (side - 1) * CC)
            rinvs.append(rinv_all[other])
        extended = jnp.concatenate(parts, axis=1)
        positions = jnp.concatenate(poss).astype(jnp.int32)
        rinv = jnp.concatenate(rinvs)
        weights = column_weights(positions, rinv, taper, CC)
        gram = gram_of(extended, weights)
        wmat = transform(gram, K)
        block = lax.dynamic_index_in_dim(ens, index, 1, keepdims=False)
        return apply_weights(wmat, block)
    out = lax.map(tile, jnp.arange(tiles, dtype=jnp.int32))
    out = jnp.transpose(out, (1, 0, 2, 3, 4))
    return out.reshape(N_LAG, tiles * CC, K, PTS)
```

```python
import jax
import jax.numpy as jnp
from jax import lax
from jax.experimental import pallas as pl
from jax.experimental.pallas import tpu as pltpu
from jax.sharding import PartitionSpec as P

NS_ITERS = 4
K = 64
U = 8
W = 2 * K
Q = 4
GRAM = U * K
HALF = GRAM // 2
SENT = HALF + 48
F32 = jnp.float32
BF16 = jnp.bfloat16
VMEM = pltpu.VMEM


def halves(x):
    high = x.astype(BF16)
    return high, (x - high.astype(F32)).astype(BF16)


def iota(shape, axis):
    return lax.broadcasted_iota(jnp.int32, shape, axis)


def encode(folded, bvec, mvec, diag):
    bhi, blo = halves(bvec)
    mhi, mlo = halves(mvec)
    rest = [x.astype(F32) for x in (bhi, blo, mhi, mlo)] + [diag, jnp.zeros_like(diag)]
    return folded.astype(BF16), jnp.concatenate(rest, axis=0).astype(BF16)


def decode(ref, at=()):
    whole = ref[at + (slice(0, HALF),)].astype(F32)
    rest = ref[at + (slice(HALF, SENT),)].astype(F32)
    return whole, rest[0:8] + rest[8:16], rest[16:24] + rest[24:32], rest[32:40]


def mix(sums_ref, taper_ref, side):
    lane = iota((1, W), 1)
    row, col = iota((K, W), 0), iota((K, W), 1) % K

    def same(f):
        return taper_ref[min(abs(2 * f), 31)]

    def crossed(f):
        return jnp.where(lane < K, taper_ref[min(abs(2 * f + 1), 31)], taper_ref[min(abs(2 * f - 1), 31)])

    out = [None] * U
    cross = {f: crossed(f) for f in range(1 - U + U * side, U + U * side)}
    for u in range(U):
        here = sums_ref[K * u : K * (u + 1), :]
        swapped = pltpu.roll(here, K, 1)
        for v in range(U):
            f = u - v + U * side
            term = here * same(f) + swapped * cross[f]
            out[v] = term if u == 0 else out[v] + term
    folded = jnp.concatenate([jnp.where(row <= col, out[v], out[v + U // 2]) for v in range(U // 2)], axis=0)
    sub = iota((U, W), 0)
    diag = jnp.zeros((U, W), F32)
    for v in range(U // 2):
        line = jnp.sum(jnp.where(row == col, out[v + U // 2], 0.0), axis=0, keepdims=True)
        diag = jnp.where(sub == v, line, diag)
    vectors = []
    for at in (GRAM, GRAM + U):
        here = sums_ref[at : at + U, :]
        swapped = pltpu.roll(here, K, 1)
        total = jnp.zeros((U, W), F32)
        for d in range(U):
            f, g = U * side - d, U * side - d + U
            turned, also = (pltpu.roll(x, d, 0) if d else x for x in (here, swapped))
            total = total + turned * jnp.where(sub >= d, same(f), same(g))
            total = total + also * jnp.where(sub >= d, crossed(f), crossed(g))
        vectors.append(total)
    return folded, vectors[0], vectors[1], diag


def store(out_ref, parts):
    folded, rest = encode(*parts)
    out_ref[0:HALF, :] = folded
    out_ref[HALF:SENT, :] = rest


def obs_kernel(count_hbm, taper_hbm, anom_hbm, innov_hbm, invv_hbm, col_hbm, sums_ref, right_ref,
               count_ref, taper_ref, anom_ref, innov_ref, invv_ref, col_ref, sems):
    pairs = ((anom_hbm, anom_ref), (innov_hbm, innov_ref), (invv_hbm, invv_ref), (col_hbm, col_ref),
             (count_hbm, count_ref), (taper_hbm, taper_ref))
    copies = [pltpu.make_async_copy(a, b, sems.at[i]) for i, (a, b) in enumerate(pairs)]
    for copy in copies:
        copy.start()
    for copy in copies:
        copy.wait()
    slots = anom_ref.shape[1]
    rinv = jnp.where(iota((1, slots), 1) < count_ref[0], invv_ref[...], 0.0)
    column = col_ref[...]
    outer, inner = column // Q, column % Q
    whole = anom_ref[...]
    mean = jnp.sum(whole, axis=0, keepdims=True) * (1.0 / K)
    anom = whole - mean
    left = [anom * jnp.where(outer == a, rinv, 0.0) for a in range(Q)]
    row = iota((16, slots), 0)
    rows = jnp.where(row < Q, innov_ref[...] * rinv, jnp.where(row < 2 * Q, mean * rinv, 0.0))
    left.append(jnp.where(row % Q == outer, rows, 0.0))
    lhi, llo = halves(jnp.concatenate(left, axis=0))
    rhi, rlo = halves(jnp.concatenate([jnp.where(inner == b, anom, 0.0) for b in range(Q)], axis=0))
    mhi, mlo = halves(jnp.where(iota((16, slots), 0) == inner, mean, 0.0))

    def dot(a, b):
        return lax.dot_general(a, b, (((1,), (1,)), ((), ())), preferred_element_type=F32)

    sums = dot(lhi, rhi) + (dot(lhi, rlo) + dot(llo, rhi))
    thi, tlo = lhi[Q * K :], llo[Q * K :]
    scalars = dot(thi, mhi) + (dot(thi, mlo) + dot(tlo, mhi))
    lane = iota((1, Q * K), 1) // K
    spread = jnp.zeros((8, Q * K), F32)
    for b in range(Q):
        spread = jnp.where(lane == b, scalars[:8, b : b + 1], spread)
    factor = jnp.where(iota((8, 1), 0) < Q, 1.0, 0.5)
    vectors = sums[Q * K : Q * K + 8] + spread * factor
    for a in range(Q):
        for i in range(2):
            u = 2 * a + i
            sums_ref[K * u : K * (u + 1), :] = sums[K * a : K * (a + 1), W * i : W * (i + 1)]
            sums_ref[GRAM + u : GRAM + u + 1, :] = vectors[a : a + 1, W * i : W * (i + 1)]
            sums_ref[GRAM + U + u : GRAM + U + u + 1, :] = vectors[Q + a : Q + a + 1, W * i : W * (i + 1)]
    store(right_ref, mix(sums_ref, taper_ref, -1))


def left_kernel(taper_ref, sums_ref, left_ref):
    store(left_ref, mix(sums_ref, taper_ref, 1))


def own_kernel(taper_ref, sums_ref, own_ref):
    folded, bvec, mvec, diag = mix(sums_ref, taper_ref, 0)
    own_ref[0:HALF, :] = folded
    own_ref[HALF : HALF + 8, :] = bvec
    own_ref[HALF + 8 : HALF + 16, :] = mvec
    own_ref[HALF + 16 : HALF + 24, :] = diag


def add_kernel(own_ref, before_ref, after_ref, out_ref):
    parts = [own_ref[0:HALF, :]] + [own_ref[HALF + 8 * i : HALF + 8 * (i + 1), :] for i in range(3)]
    for ref in (before_ref, after_ref):
        parts = [x + y for x, y in zip(parts, decode(ref))]
    store(out_ref, parts)


def members_kernel(ens_ref, mean_ref, anom_ref):
    for c in range(ens_ref.shape[0]):
        members = ens_ref[c].astype(F32)
        mean = jnp.sum(members, axis=0, keepdims=True) * (1.0 / K)
        mean_ref[c : c + 1, :] = mean
        anom_ref[K * c : K * (c + 1), :] = (members - mean).astype(BF16)


def finish_kernel(parts_ref, mean_ref, anom_ref, out_ref, buf, sems):
    width = Q * K
    groups = U * W // width
    lane = iota((1, width), 1) // K
    diagonal = iota((width, width), 0) // K == iota((width, width), 1) // K
    eye = jnp.where(iota((K, width), 0) == iota((K, width), 1) % K, 1.0, 0.0)
    row, col = iota((K, W), 0), iota((K, W), 1) % K

    def spread(x):
        tall = jnp.concatenate([x] * Q, axis=0)
        return jnp.where(diagonal, tall, jnp.zeros_like(tall))

    def dot(a, b):
        return jnp.dot(a, b, preferred_element_type=F32)

    def times(left, right):
        n = len(left)
        parts = [halves(x) for x in left]
        hi = [p[0] for p in parts]
        lo = [p[1] for p in parts]
        rhi, rlo = halves(right)
        first = dot(jnp.concatenate(hi + lo, axis=0), spread(rhi))
        second = dot(jnp.concatenate(hi, axis=0), spread(rlo))
        out = first[: n * K] + (first[n * K :] + second)
        return [out[i * K : (i + 1) * K] for i in range(n)]

    def lane_sums(x):
        out = jnp.zeros_like(x)
        for cc in range(Q):
            out = jnp.where(lane == cc, jnp.sum(jnp.where(lane == cc, x, 0.0), axis=1, keepdims=True), out)
        return out

    folded, bvec, mvec, diag = decode(parts_ref, (0,))
    for lag in range(1, parts_ref.shape[0]):
        more = decode(parts_ref, (lag,))
        folded, bvec, mvec, diag = folded + more[0], bvec + more[1], mvec + more[2], diag + more[3]
    units = [None] * U
    for v in range(U // 2):
        here = folded[K * v : K * (v + 1)]
        tall = jnp.transpose(here)
        turned = jnp.concatenate([tall[:K], tall[K:]], axis=1)
        units[v] = jnp.where(row <= col, here, turned)
        units[v + U // 2] = jnp.where(row == col, diag[v : v + 1], jnp.where(row > col, here, turned))
    pairs = [slice(2 * g, 2 * g + 2) for g in range(groups)]

    def wide(vec, g):
        return jnp.concatenate([vec[2 * g : 2 * g + 1], vec[2 * g + 1 : 2 * g + 2]], axis=1)

    bvec = [wide(bvec, g) for g in range(groups)]
    mvec = [wide(mvec, g) for g in range(groups)]
    amat = [
        jnp.concatenate(units[pairs[g]], axis=1) + mvec[g] + lane_sums(eye * mvec[g]) + (K - 1.0) * eye
        for g in range(groups)
    ]
    scale = [jnp.sqrt(lane_sums(jnp.sum(a * a, axis=0, keepdims=True))) for a in amat]
    yval = [a / s for a, s in zip(amat, scale)]
    mval = [1.5 * eye - 0.5 * y for y in yval]
    zval = mval
    yval = [times([y], m)[0] for y, m in zip(yval, mval)]
    for step in range(1, NS_ITERS):
        prod = [times([z], y)[0] for z, y in zip(zval, yval)]
        mval = [1.5 * eye - 0.5 * p for p in prod]
        if step < NS_ITERS - 1:
            both = [times([y, z], m) for y, z, m in zip(yval, zval, mval)]
            yval, zval = [b[0] for b in both], [b[1] for b in both]
        else:
            zval = [times([z], m)[0] for z, m in zip(zval, mval)]
    weights = []
    for g in range(groups):
        inner = lane_sums(zval[g] * bvec[g])
        shift = jnp.sum(zval[g] * inner, axis=0, keepdims=True) / scale[g]
        weights.append((zval[g] * (jnp.sqrt(K - 1.0) / jnp.sqrt(scale[g])) + shift).astype(BF16))
    copies = []
    for g in range(groups):
        mixed = dot(spread(weights[g]), anom_ref[width * g : width * (g + 1), :])
        for cc in range(Q):
            c = Q * g + cc
            buf[c] = (mean_ref[c : c + 1, :] + mixed[K * cc : K * (cc + 1)]).astype(BF16)
        copies.append(pltpu.make_async_copy(buf.at[pl.ds(Q * g, Q)], out_ref.at[pl.ds(Q * g, Q)], sems.at[g]))
        copies[-1].start()
    for copy in copies:
        copy.wait()


def on_device(ensemble, obs_anomaly, innovation, inv_variance, obs_column, obs_count, taper):
    slots = obs_anomaly.shape[1]
    _, ncol, _, points = ensemble.shape
    vmem = pl.BlockSpec(memory_space=VMEM)
    smem = pl.BlockSpec(memory_space=pltpu.SMEM)
    hbm = pl.BlockSpec(memory_space=pltpu.HBM)
    params = pltpu.CompilerParams(vmem_limit_bytes=48 * 2**20)
    sent = jax.ShapeDtypeStruct((SENT, W), BF16)

    def cost(flops):
        return pl.CostEstimate(flops=flops, bytes_accessed=2**19, transcendentals=0)

    sums, right = pl.pallas_call(
        obs_kernel,
        out_shape=[jax.ShapeDtypeStruct((GRAM + 2 * U, W), F32), sent],
        in_specs=[hbm] * 6,
        out_specs=[vmem, vmem],
        scratch_shapes=[
            pltpu.SMEM((1,), jnp.int32),
            pltpu.SMEM(taper.shape, F32),
            VMEM(obs_anomaly.shape, F32),
            VMEM((1, slots), F32),
            VMEM((1, slots), F32),
            VMEM((1, slots), jnp.int32),
            pltpu.SemaphoreType.DMA((6,)),
        ],
        compiler_params=params,
        name="obs_sums",
    )(obs_count, taper, obs_anomaly, innovation[None], inv_variance[None], obs_column[None])
    count = lax.axis_size("space")
    before = lax.ppermute(right, "space", [(i, (i + 1) % count) for i in range(count)])
    left = pl.pallas_call(
        left_kernel,
        out_shape=sent,
        in_specs=[smem, vmem],
        out_specs=vmem,
        compiler_params=params,
        cost_estimate=cost(10**8),
        name="left_sums",
    )(taper, sums)
    after = lax.ppermute(left, "space", [((i + 1) % count, i) for i in range(count)])
    own = pl.pallas_call(
        own_kernel,
        out_shape=jax.ShapeDtypeStruct((HALF + 24, W), F32),
        in_specs=[smem, vmem],
        out_specs=vmem,
        compiler_params=params,
        cost_estimate=cost(10**8),
        name="own_sums",
    )(taper, sums)
    mean, anomalies = pl.pallas_call(
        members_kernel,
        out_shape=[jax.ShapeDtypeStruct((ncol, points), F32), jax.ShapeDtypeStruct((ncol * K, points), BF16)],
        in_specs=[vmem],
        out_specs=[vmem, vmem],
        compiler_params=params,
        cost_estimate=cost(10**8),
        name="member_means",
    )(ensemble[0])
    mixed = pl.pallas_call(
        add_kernel,
        out_shape=sent,
        in_specs=[vmem] * 3,
        out_specs=vmem,
        compiler_params=params,
        name="add_sides",
    )(own, before, after)
    parts = lax.all_gather(mixed, "lag")
    out = pl.pallas_call(
        finish_kernel,
        out_shape=jax.ShapeDtypeStruct((ncol, K, points), BF16),
        in_specs=[vmem] * 3,
        out_specs=pl.BlockSpec(memory_space=pl.ANY),
        scratch_shapes=[VMEM((ncol, K, points), BF16), pltpu.SemaphoreType.DMA((ncol // Q,))],
        compiler_params=params,
        name="transform_apply",
    )(parts, mean, anomalies)
    return out[None]


def solution(mesh):
    placed = (
        P("lag", "space", None, None),
        P(None, ("space", "lag")),
        P(("space", "lag")),
        P(("space", "lag")),
        P(("space", "lag")),
        P(("space", "lag")),
        P(),
    )
    return jax.shard_map(
        on_device,
        mesh=mesh,
        in_specs=placed,
        out_specs=P("lag", "space", None, None),
        check_vma=False,
    )
```

```python
import jax
import jax.numpy as jnp
from jax import lax
from jax.experimental import pallas as pl
from jax.experimental.pallas import tpu as pltpu
from jax.sharding import PartitionSpec as P

NS_ITERS = 4
K = 64
REACH = 32
U = 8
W = 2 * K
Q = 4
GRAM = U * K
HALF = GRAM // 2
SENT = HALF + 48
F32 = jnp.float32
BF16 = jnp.bfloat16
VMEM = pltpu.VMEM


def halves(x):
    high = x.astype(BF16)
    return high, (x - high.astype(F32)).astype(BF16)


def iota(shape, axis):
    return lax.broadcasted_iota(jnp.int32, shape, axis)


def encode(folded, bvec, mvec, diag):
    bhi, blo = halves(bvec)
    mhi, mlo = halves(mvec)
    rest = [x.astype(F32) for x in (bhi, blo, mhi, mlo)] + [diag, jnp.zeros_like(diag)]
    return folded.astype(BF16), jnp.concatenate(rest, axis=0).astype(BF16)


def decode(ref, at=()):
    whole = ref[at + (slice(0, HALF),)].astype(F32)
    rest = ref[at + (slice(HALF, SENT),)].astype(F32)
    return whole, rest[0:8] + rest[8:16], rest[16:24] + rest[24:32], rest[32:40]


def mix(sums_ref, taper_ref, side):
    lane = iota((1, W), 1)
    row, col = iota((K, W), 0), iota((K, W), 1) % K

    def at(distance):
        d = min(abs(distance), REACH - 1)
        return taper_ref[d : d + 1, :]

    def same(f):
        return at(2 * f)

    def crossed(f):
        return jnp.where(lane < K, at(2 * f + 1), at(2 * f - 1))

    out = [None] * U
    cross = {f: crossed(f) for f in range(1 - U + U * side, U + U * side)}
    for u in range(U):
        here = sums_ref[K * u : K * (u + 1), :]
        swapped = pltpu.roll(here, K, 1)
        for v in range(U):
            f = u - v + U * side
            term = here * same(f) + swapped * cross[f]
            out[v] = term if u == 0 else out[v] + term
    folded = jnp.concatenate([jnp.where(row <= col, out[v], out[v + U // 2]) for v in range(U // 2)], axis=0)
    sub = iota((U, W), 0)
    diag = jnp.zeros((U, W), F32)
    for v in range(U // 2):
        line = jnp.sum(jnp.where(row == col, out[v + U // 2], 0.0), axis=0, keepdims=True)
        diag = jnp.where(sub == v, line, diag)
    vectors = []
    for start in (GRAM, GRAM + U):
        here = sums_ref[start : start + U, :]
        swapped = pltpu.roll(here, K, 1)
        total = jnp.zeros((U, W), F32)
        for d in range(U):
            f, g = U * side - d, U * side - d + U
            turned, also = (pltpu.roll(x, d, 0) if d else x for x in (here, swapped))
            total = total + turned * jnp.where(sub >= d, same(f), same(g))
            total = total + also * jnp.where(sub >= d, crossed(f), crossed(g))
        vectors.append(total)
    return folded, vectors[0], vectors[1], diag


def store(out_ref, parts):
    folded, rest = encode(*parts)
    out_ref[0:HALF, :] = folded
    out_ref[HALF:SENT, :] = rest


def obs_kernel(count_ref, taper_hbm, anom_hbm, innov_hbm, invv_hbm, col_hbm, sums_ref, table_ref, right_ref,
               taper_ref, anom_ref, innov_ref, invv_ref, col_ref, sems):
    pairs = ((anom_hbm, anom_ref), (innov_hbm, innov_ref), (invv_hbm, invv_ref), (col_hbm, col_ref),
             (taper_hbm, taper_ref))
    copies = [pltpu.make_async_copy(a, b, sems.at[i]) for i, (a, b) in enumerate(pairs)]
    for copy in copies:
        copy.start()
    for copy in copies:
        copy.wait()
    slots = anom_ref.shape[1]
    rinv = jnp.where(iota((1, slots), 1) < count_ref[0], invv_ref[...], 0.0)
    column = col_ref[...]
    outer, inner = column // Q, column % Q
    whole = anom_ref[...]
    mean = jnp.sum(whole, axis=0, keepdims=True) * (1.0 / K)
    anom = whole - mean
    left = [anom * jnp.where(outer == a, rinv, 0.0) for a in range(Q)]
    row = iota((16, slots), 0)
    rows = jnp.where(row < Q, innov_ref[...] * rinv, jnp.where(row < 2 * Q, mean * rinv, 0.0))
    left.append(jnp.where(row % Q == outer, rows, 0.0))
    lhi, llo = halves(jnp.concatenate(left, axis=0))
    rhi, rlo = halves(jnp.concatenate([jnp.where(inner == b, anom, 0.0) for b in range(Q)], axis=0))
    mhi, mlo = halves(jnp.where(iota((16, slots), 0) == inner, mean, 0.0))

    def dot(a, b):
        return lax.dot_general(a, b, (((1,), (1,)), ((), ())), preferred_element_type=F32)

    sums = dot(lhi, rhi) + (dot(lhi, rlo) + dot(llo, rhi))
    thi, tlo = lhi[Q * K :], llo[Q * K :]
    scalars = dot(thi, mhi) + (dot(thi, mlo) + dot(tlo, mhi))
    lane = iota((1, Q * K), 1) // K
    spread = jnp.zeros((8, Q * K), F32)
    for b in range(Q):
        spread = jnp.where(lane == b, scalars[:8, b : b + 1], spread)
    factor = jnp.where(iota((8, 1), 0) < Q, 1.0, 0.5)
    vectors = sums[Q * K : Q * K + 8] + spread * factor
    for a in range(Q):
        for i in range(2):
            u = 2 * a + i
            sums_ref[K * u : K * (u + 1), :] = sums[K * a : K * (a + 1), W * i : W * (i + 1)]
            sums_ref[GRAM + u : GRAM + u + 1, :] = vectors[a : a + 1, W * i : W * (i + 1)]
            sums_ref[GRAM + U + u : GRAM + U + u + 1, :] = vectors[Q + a : Q + a + 1, W * i : W * (i + 1)]
    for d in range(REACH):
        table_ref[d : d + 1, :] = jnp.full((1, W), taper_ref[d], F32)
    store(right_ref, mix(sums_ref, table_ref, -1))


def left_kernel(taper_ref, sums_ref, left_ref):
    store(left_ref, mix(sums_ref, taper_ref, 1))


def put(out_ref, parts):
    folded, bvec, mvec, diag = parts
    out_ref[0:HALF, :] = folded
    out_ref[HALF : HALF + 8, :] = bvec
    out_ref[HALF + 8 : HALF + 16, :] = mvec
    out_ref[HALF + 16 : HALF + 24, :] = diag


def get(ref):
    return [ref[0:HALF, :]] + [ref[HALF + 8 * i : HALF + 8 * (i + 1), :] for i in range(3)]


def own_kernel(taper_ref, sums_ref, own_ref):
    put(own_ref, mix(sums_ref, taper_ref, 0))


def before_kernel(own_ref, before_ref, out_ref):
    put(out_ref, [x + y for x, y in zip(get(own_ref), decode(before_ref))])


def after_kernel(own_ref, after_ref, out_ref):
    store(out_ref, [x + y for x, y in zip(get(own_ref), decode(after_ref))])


def members_kernel(ens_ref, mean_ref, anom_ref):
    for c in range(ens_ref.shape[0]):
        members = ens_ref[c].astype(F32)
        mean = jnp.sum(members, axis=0, keepdims=True) * (1.0 / K)
        mean_ref[c : c + 1, :] = mean
        anom_ref[K * c : K * (c + 1), :] = (members - mean).astype(BF16)


def finish_kernel(parts_ref, mean_ref, anom_ref, out_ref, buf, sems):
    width = Q * K
    groups = U * W // width
    lane = iota((1, width), 1) // K
    diagonal = iota((width, width), 0) // K == iota((width, width), 1) // K
    eye = jnp.where(iota((K, width), 0) == iota((K, width), 1) % K, 1.0, 0.0)
    row, col = iota((K, W), 0), iota((K, W), 1) % K

    def spread(x):
        tall = jnp.concatenate([x] * Q, axis=0)
        return jnp.where(diagonal, tall, jnp.zeros_like(tall))

    def dot(a, b):
        return jnp.dot(a, b, preferred_element_type=F32)

    def times(left, right):
        n = len(left)
        parts = [halves(x) for x in left]
        hi = [p[0] for p in parts]
        lo = [p[1] for p in parts]
        rhi, rlo = halves(right)
        first = dot(jnp.concatenate(hi + lo, axis=0), spread(rhi))
        second = dot(jnp.concatenate(hi, axis=0), spread(rlo))
        out = first[: n * K] + (first[n * K :] + second)
        return [out[i * K : (i + 1) * K] for i in range(n)]

    def lane_sums(x):
        out = jnp.zeros_like(x)
        for cc in range(Q):
            out = jnp.where(lane == cc, jnp.sum(jnp.where(lane == cc, x, 0.0), axis=1, keepdims=True), out)
        return out

    folded, bvec, mvec, diag = decode(parts_ref, (0,))
    for lag in range(1, parts_ref.shape[0]):
        more = decode(parts_ref, (lag,))
        folded, bvec, mvec, diag = folded + more[0], bvec + more[1], mvec + more[2], diag + more[3]
    units = [None] * U
    for v in range(U // 2):
        here = folded[K * v : K * (v + 1)]
        tall = jnp.transpose(here)
        turned = jnp.concatenate([tall[:K], tall[K:]], axis=1)
        units[v] = jnp.where(row <= col, here, turned)
        units[v + U // 2] = jnp.where(row == col, diag[v : v + 1], jnp.where(row > col, here, turned))
    pairs = [slice(2 * g, 2 * g + 2) for g in range(groups)]

    def wide(vec, g):
        return jnp.concatenate([vec[2 * g : 2 * g + 1], vec[2 * g + 1 : 2 * g + 2]], axis=1)

    bvec = [wide(bvec, g) for g in range(groups)]
    mvec = [wide(mvec, g) for g in range(groups)]
    amat = [
        jnp.concatenate(units[pairs[g]], axis=1) + mvec[g] + lane_sums(eye * mvec[g]) + (K - 1.0) * eye
        for g in range(groups)
    ]
    scale = [jnp.sqrt(lane_sums(jnp.sum(a * a, axis=0, keepdims=True))) for a in amat]
    yval = [a / s for a, s in zip(amat, scale)]
    mval = [1.5 * eye - 0.5 * y for y in yval]
    zval = mval
    yval = [times([y], m)[0] for y, m in zip(yval, mval)]
    for step in range(1, NS_ITERS):
        prod = [times([z], y)[0] for z, y in zip(zval, yval)]
        mval = [1.5 * eye - 0.5 * p for p in prod]
        if step < NS_ITERS - 1:
            both = [times([y, z], m) for y, z, m in zip(yval, zval, mval)]
            yval, zval = [b[0] for b in both], [b[1] for b in both]
        else:
            zval = [times([z], m)[0] for z, m in zip(zval, mval)]
    weights = []
    for g in range(groups):
        inner = lane_sums(zval[g] * bvec[g])
        shift = jnp.sum(zval[g] * inner, axis=0, keepdims=True) / scale[g]
        weights.append((zval[g] * (jnp.sqrt(K - 1.0) / jnp.sqrt(scale[g])) + shift).astype(BF16))
    copies = []
    for g in range(groups):
        mixed = dot(spread(weights[g]), anom_ref[width * g : width * (g + 1), :])
        for cc in range(Q):
            c = Q * g + cc
            buf[c] = (mean_ref[c : c + 1, :] + mixed[K * cc : K * (cc + 1)]).astype(BF16)
        copies.append(pltpu.make_async_copy(buf.at[pl.ds(Q * g, Q)], out_ref.at[pl.ds(Q * g, Q)], sems.at[g]))
        copies[-1].start()
    for copy in copies:
        copy.wait()


def on_device(ensemble, obs_anomaly, innovation, inv_variance, obs_column, obs_count, taper):
    slots = obs_anomaly.shape[1]
    _, ncol, _, points = ensemble.shape
    vmem = pl.BlockSpec(memory_space=VMEM)
    smem = pl.BlockSpec(memory_space=pltpu.SMEM)
    hbm = pl.BlockSpec(memory_space=pltpu.HBM)
    params = pltpu.CompilerParams(vmem_limit_bytes=48 * 2**20)
    sent = jax.ShapeDtypeStruct((SENT, W), BF16)
    kept = jax.ShapeDtypeStruct((HALF + 24, W), F32)

    def cost(flops):
        return pl.CostEstimate(flops=flops, bytes_accessed=2**19, transcendentals=0)

    observed = (taper, obs_anomaly, innovation[None], inv_variance[None], obs_column[None])
    sums, table, right = pl.pallas_call(
        obs_kernel,
        out_shape=[jax.ShapeDtypeStruct((GRAM + 2 * U, W), F32), jax.ShapeDtypeStruct((REACH, W), F32), sent],
        in_specs=[smem] + [hbm] * 5,
        out_specs=[vmem] * 3,
        scratch_shapes=[
            pltpu.SMEM(taper.shape, F32),
            VMEM(obs_anomaly.shape, F32),
            VMEM((1, slots), F32),
            VMEM((1, slots), F32),
            VMEM((1, slots), jnp.int32),
            pltpu.SemaphoreType.DMA((5,)),
        ],
        compiler_params=params,
        name="obs_sums",
    )(obs_count, *(pltpu.with_memory_space_constraint(x, pltpu.HBM) for x in observed))
    count = lax.axis_size("space")
    before = lax.ppermute(right, "space", [(i, (i + 1) % count) for i in range(count)])
    left = pl.pallas_call(
        left_kernel,
        out_shape=sent,
        in_specs=[vmem, vmem],
        out_specs=vmem,
        compiler_params=params,
        cost_estimate=cost(10**8),
        name="left_sums",
    )(table, sums)
    after = lax.ppermute(left, "space", [((i + 1) % count, i) for i in range(count)])
    own = pl.pallas_call(
        own_kernel,
        out_shape=kept,
        in_specs=[vmem, vmem],
        out_specs=vmem,
        compiler_params=params,
        cost_estimate=cost(10**8),
        name="own_sums",
    )(table, sums)
    mean, anomalies = pl.pallas_call(
        members_kernel,
        out_shape=[jax.ShapeDtypeStruct((ncol, points), F32), jax.ShapeDtypeStruct((ncol * K, points), BF16)],
        in_specs=[vmem],
        out_specs=[vmem, vmem],
        compiler_params=params,
        cost_estimate=cost(10**8),
        name="member_means",
    )(ensemble[0])
    own = pl.pallas_call(
        before_kernel,
        out_shape=kept,
        in_specs=[vmem] * 2,
        out_specs=vmem,
        compiler_params=params,
        name="add_before",
    )(own, before)
    mixed = pl.pallas_call(
        after_kernel,
        out_shape=sent,
        in_specs=[vmem] * 2,
        out_specs=vmem,
        compiler_params=params,
        name="add_after",
    )(own, after)
    parts = lax.all_gather(mixed, "lag")
    out = pl.pallas_call(
        finish_kernel,
        out_shape=jax.ShapeDtypeStruct((ncol, K, points), BF16),
        in_specs=[vmem] * 3,
        out_specs=pl.BlockSpec(memory_space=pl.ANY),
        scratch_shapes=[VMEM((ncol, K, points), BF16), pltpu.SemaphoreType.DMA((ncol // Q,))],
        compiler_params=params,
        name="transform_apply",
    )(parts, mean, anomalies)
    return out[None]


def solution(mesh):
    placed = (
        P("lag", "space", None, None),
        P(None, ("space", "lag")),
        P(("space", "lag")),
        P(("space", "lag")),
        P(("space", "lag")),
        P(("space", "lag")),
        P(),
    )
    return jax.shard_map(
        on_device,
        mesh=mesh,
        in_specs=placed,
        out_specs=P("lag", "space", None, None),
        check_vma=False,
    )
```

```python
import jax
import jax.numpy as jnp
from jax import lax
from jax.experimental import pallas as pl
from jax.experimental.pallas import tpu as pltpu
from jax.sharding import PartitionSpec as P

NS_ITERS = 4
K = 64
REACH = 32
U = 8
W = 2 * K
Q = 4
GRAM = U * K
HALF = GRAM // 2
SENT = HALF + 48
F32 = jnp.float32
BF16 = jnp.bfloat16
VMEM = pltpu.VMEM


def halves(x):
    high = x.astype(BF16)
    return high, (x - high.astype(F32)).astype(BF16)


def iota(shape, axis):
    return lax.broadcasted_iota(jnp.int32, shape, axis)


def encode(folded, bvec, mvec, diag):
    bhi, blo = halves(bvec)
    mhi, mlo = halves(mvec)
    rest = [x.astype(F32) for x in (bhi, blo, mhi, mlo)] + [diag, jnp.zeros_like(diag)]
    return folded.astype(BF16), jnp.concatenate(rest, axis=0).astype(BF16)


def decode(ref, at=()):
    whole = ref[at + (slice(0, HALF),)].astype(F32)
    rest = ref[at + (slice(HALF, SENT),)].astype(F32)
    return whole, rest[0:8] + rest[8:16], rest[16:24] + rest[24:32], rest[32:40]


def mix(sums_ref, taper_ref, side):
    lane = iota((1, W), 1)
    row, col = iota((K, W), 0), iota((K, W), 1) % K

    def at(distance):
        d = min(abs(distance), REACH - 1)
        return taper_ref[d : d + 1, :]

    def same(f):
        return at(2 * f)

    def crossed(f):
        return jnp.where(lane < K, at(2 * f + 1), at(2 * f - 1))

    out = [None] * U
    cross = {f: crossed(f) for f in range(1 - U + U * side, U + U * side)}
    for u in range(U):
        here = sums_ref[K * u : K * (u + 1), :]
        swapped = pltpu.roll(here, K, 1)
        for v in range(U):
            f = u - v + U * side
            term = here * same(f) + swapped * cross[f]
            out[v] = term if u == 0 else out[v] + term
    folded = jnp.concatenate([jnp.where(row <= col, out[v], out[v + U // 2]) for v in range(U // 2)], axis=0)
    sub = iota((U, W), 0)
    diag = jnp.zeros((U, W), F32)
    for v in range(U // 2):
        line = jnp.sum(jnp.where(row == col, out[v + U // 2], 0.0), axis=0, keepdims=True)
        diag = jnp.where(sub == v, line, diag)
    vectors = []
    for start in (GRAM, GRAM + U):
        here = sums_ref[start : start + U, :]
        swapped = pltpu.roll(here, K, 1)
        total = jnp.zeros((U, W), F32)
        for d in range(U):
            f, g = U * side - d, U * side - d + U
            turned, also = (pltpu.roll(x, d, 0) if d else x for x in (here, swapped))
            total = total + turned * jnp.where(sub >= d, same(f), same(g))
            total = total + also * jnp.where(sub >= d, crossed(f), crossed(g))
        vectors.append(total)
    return folded, vectors[0], vectors[1], diag


def store(out_ref, parts):
    folded, rest = encode(*parts)
    out_ref[0:HALF, :] = folded
    out_ref[HALF:SENT, :] = rest


def obs_kernel(count_ref, taper_hbm, anom_hbm, innov_hbm, invv_hbm, col_hbm, sums_ref, table_ref, right_ref,
               taper_ref, anom_ref, innov_ref, invv_ref, col_ref, sems):
    pairs = ((anom_hbm, anom_ref), (innov_hbm, innov_ref), (invv_hbm, invv_ref), (col_hbm, col_ref),
             (taper_hbm, taper_ref))
    copies = [pltpu.make_async_copy(a, b, sems.at[i]) for i, (a, b) in enumerate(pairs)]
    for copy in copies:
        copy.start()
    for copy in copies[1:]:
        copy.wait()
    slots = anom_ref.shape[1]
    for d in range(REACH):
        table_ref[d : d + 1, :] = jnp.full((1, W), taper_ref[d], F32)
    rinv = jnp.where(iota((1, slots), 1) < count_ref[0], invv_ref[...], 0.0)
    column = col_ref[...]
    outer, inner = column // Q, column % Q
    scaled = [jnp.where(outer == a, rinv, 0.0) for a in range(Q)]
    copies[0].wait()
    whole = anom_ref[...]
    mean = jnp.sum(whole, axis=0, keepdims=True) * (1.0 / K)
    anom = whole - mean
    left = [anom * scaled[a] for a in range(Q)]
    row = iota((16, slots), 0)
    rows = jnp.where(row < Q, innov_ref[...] * rinv, jnp.where(row < 2 * Q, mean * rinv, 0.0))
    left.append(jnp.where(row % Q == outer, rows, 0.0))
    lhi, llo = halves(jnp.concatenate(left, axis=0))
    rhi, rlo = halves(jnp.concatenate([jnp.where(inner == b, anom, 0.0) for b in range(Q)], axis=0))
    mhi, mlo = halves(jnp.where(iota((16, slots), 0) == inner, mean, 0.0))

    def dot(a, b):
        return lax.dot_general(a, b, (((1,), (1,)), ((), ())), preferred_element_type=F32)

    n = Q * K + 16
    both = dot(jnp.concatenate([lhi, llo], axis=0), rhi)
    sums = both[:n] + (both[n:] + dot(lhi, rlo))
    thi, tlo = lhi[Q * K :], llo[Q * K :]
    scalars = dot(thi, mhi) + (dot(thi, mlo) + dot(tlo, mhi))
    lane = iota((1, Q * K), 1) // K
    spread = jnp.zeros((8, Q * K), F32)
    for b in range(Q):
        spread = jnp.where(lane == b, scalars[:8, b : b + 1], spread)
    factor = jnp.where(iota((8, 1), 0) < Q, 1.0, 0.5)
    vectors = sums[Q * K : Q * K + 8] + spread * factor
    for a in range(Q):
        for i in range(2):
            u = 2 * a + i
            sums_ref[K * u : K * (u + 1), :] = sums[K * a : K * (a + 1), W * i : W * (i + 1)]
            sums_ref[GRAM + u : GRAM + u + 1, :] = vectors[a : a + 1, W * i : W * (i + 1)]
            sums_ref[GRAM + U + u : GRAM + U + u + 1, :] = vectors[Q + a : Q + a + 1, W * i : W * (i + 1)]
    store(right_ref, mix(sums_ref, table_ref, -1))


def left_kernel(taper_ref, sums_ref, left_ref):
    store(left_ref, mix(sums_ref, taper_ref, 1))


def put(out_ref, parts):
    folded, bvec, mvec, diag = parts
    out_ref[0:HALF, :] = folded
    out_ref[HALF : HALF + 8, :] = bvec
    out_ref[HALF + 8 : HALF + 16, :] = mvec
    out_ref[HALF + 16 : HALF + 24, :] = diag


def get(ref):
    return [ref[0:HALF, :]] + [ref[HALF + 8 * i : HALF + 8 * (i + 1), :] for i in range(3)]


def own_kernel(taper_ref, sums_ref, own_ref):
    put(own_ref, mix(sums_ref, taper_ref, 0))


def before_kernel(own_ref, before_ref, out_ref):
    put(out_ref, [x + y for x, y in zip(get(own_ref), decode(before_ref))])


def after_kernel(own_ref, after_ref, out_ref):
    store(out_ref, [x + y for x, y in zip(get(own_ref), decode(after_ref))])


def members_kernel(ens_ref, mean_ref, anom_ref):
    for c in range(ens_ref.shape[0]):
        members = ens_ref[c].astype(F32)
        mean = jnp.sum(members, axis=0, keepdims=True) * (1.0 / K)
        mean_ref[c : c + 1, :] = mean
        anom_ref[K * c : K * (c + 1), :] = (members - mean).astype(BF16)


def finish_kernel(parts_ref, mean_ref, anom_ref, out_ref, buf, sems):
    width = W
    groups = U
    n = W // K
    lane = iota((1, width), 1) // K
    diagonal = iota((width, width), 0) // K == iota((width, width), 1) // K
    eye = jnp.where(iota((K, width), 0) == iota((K, width), 1) % K, 1.0, 0.0)
    row, col = iota((K, W), 0), iota((K, W), 1) % K
    left_half = iota((K, W), 1) < K

    def spread(x):
        tall = jnp.concatenate([x] * n, axis=0)
        return jnp.where(diagonal, tall, jnp.zeros_like(tall))

    def dot(a, b):
        return jnp.dot(a, b, preferred_element_type=F32)

    def times(left, right):
        count = len(left)
        parts = [halves(x) for x in left]
        hi = [p[0] for p in parts]
        lo = [p[1] for p in parts]
        rhi, rlo = halves(right)
        first = dot(jnp.concatenate(hi + lo, axis=0), spread(rhi))
        second = dot(jnp.concatenate(hi, axis=0), spread(rlo))
        out = first[: count * K] + (first[count * K :] + second)
        return [out[i * K : (i + 1) * K] for i in range(count)]

    def lane_sums(x):
        out = jnp.zeros_like(x)
        for cc in range(n):
            out = jnp.where(lane == cc, jnp.sum(jnp.where(lane == cc, x, 0.0), axis=1, keepdims=True), out)
        return out

    folded, bvec, mvec, diag = decode(parts_ref, (0,))
    for lag in range(1, parts_ref.shape[0]):
        more = decode(parts_ref, (lag,))
        folded, bvec, mvec, diag = folded + more[0], bvec + more[1], mvec + more[2], diag + more[3]
    units = [None] * U
    for v in range(U // 2):
        here = folded[K * v : K * (v + 1)]
        if v % 2 == 0:
            square = jnp.transpose(folded[K * v : K * (v + 2)])
            upper, lower = square[:K], square[K:]
            turned = jnp.where(left_half, upper, pltpu.roll(lower, K, 1))
        else:
            turned = jnp.where(left_half, pltpu.roll(upper, K, 1), lower)
        units[v] = jnp.where(row <= col, here, turned)
        units[v + U // 2] = jnp.where(row == col, diag[v : v + 1], jnp.where(row > col, here, turned))
    bvec = [bvec[g : g + 1] for g in range(groups)]
    mvec = [mvec[g : g + 1] for g in range(groups)]
    parts = []
    for g in range(groups):
        line = eye * mvec[g]
        high, low = halves(line)
        parts += [high, low, (line - high.astype(F32) - low.astype(F32)).astype(BF16)]
    ones = jnp.where(diagonal, 1.0, 0.0).astype(BF16)
    across = dot(jnp.concatenate(parts, axis=0), ones)
    across = [sum(across[K * (3 * g + i) : K * (3 * g + i + 1)] for i in range(3)) for g in range(groups)]
    amat = [
        units[g] + mvec[g] + across[g] + (K - 1.0) * eye
        for g in range(groups)
    ]
    norms = jnp.concatenate([jnp.sum(a * a, axis=0, keepdims=True) for a in amat], axis=0)
    scale = jnp.sqrt(lane_sums(norms))
    scale = [scale[g : g + 1] for g in range(groups)]
    yval = [a / s for a, s in zip(amat, scale)]
    mval = [1.5 * eye - 0.5 * y for y in yval]
    zval = mval
    yval = [times([y], m)[0] for y, m in zip(yval, mval)]
    for step in range(1, NS_ITERS):
        prod = [times([z], y)[0] for z, y in zip(zval, yval)]
        mval = [1.5 * eye - 0.5 * p for p in prod]
        if step < NS_ITERS - 1:
            both = [times([y, z], m) for y, z, m in zip(yval, zval, mval)]
            yval, zval = [b[0] for b in both], [b[1] for b in both]
        else:
            zval = [times([z], m)[0] for z, m in zip(zval, mval)]
    weights = []
    for g in range(groups):
        inner = lane_sums(zval[g] * bvec[g])
        shift = jnp.sum(zval[g] * inner, axis=0, keepdims=True) / scale[g]
        weights.append((zval[g] * (jnp.sqrt(K - 1.0) / jnp.sqrt(scale[g])) + shift).astype(BF16))
    copies = []
    for g in range(groups):
        mixed = dot(spread(weights[g]), anom_ref[width * g : width * (g + 1), :])
        for cc in range(n):
            c = n * g + cc
            buf[c] = (mean_ref[c : c + 1, :] + mixed[K * cc : K * (cc + 1)]).astype(BF16)
        copies.append(pltpu.make_async_copy(buf.at[pl.ds(n * g, n)], out_ref.at[pl.ds(n * g, n)], sems.at[g]))
        copies[-1].start()
    for copy in copies:
        copy.wait()


def on_device(ensemble, obs_anomaly, innovation, inv_variance, obs_column, obs_count, taper):
    slots = obs_anomaly.shape[1]
    _, ncol, _, points = ensemble.shape
    vmem = pl.BlockSpec(memory_space=VMEM)
    smem = pl.BlockSpec(memory_space=pltpu.SMEM)
    hbm = pl.BlockSpec(memory_space=pltpu.HBM)
    params = pltpu.CompilerParams(vmem_limit_bytes=48 * 2**20)
    sent = jax.ShapeDtypeStruct((SENT, W), BF16)
    kept = jax.ShapeDtypeStruct((HALF + 24, W), F32)

    def cost(flops):
        return pl.CostEstimate(flops=flops, bytes_accessed=2**19, transcendentals=0)

    observed = (taper, obs_anomaly, innovation[None], inv_variance[None], obs_column[None])
    sums, table, right = pl.pallas_call(
        obs_kernel,
        out_shape=[jax.ShapeDtypeStruct((GRAM + 2 * U, W), F32), jax.ShapeDtypeStruct((REACH, W), F32), sent],
        in_specs=[smem] + [hbm] * 5,
        out_specs=[vmem] * 3,
        scratch_shapes=[
            pltpu.SMEM(taper.shape, F32),
            VMEM(obs_anomaly.shape, F32),
            VMEM((1, slots), F32),
            VMEM((1, slots), F32),
            VMEM((1, slots), jnp.int32),
            pltpu.SemaphoreType.DMA((5,)),
        ],
        compiler_params=params,
        name="obs_sums",
    )(obs_count, *(pltpu.with_memory_space_constraint(x, pltpu.HBM) for x in observed))
    count = lax.axis_size("space")
    before = lax.ppermute(right, "space", [(i, (i + 1) % count) for i in range(count)])
    left = pl.pallas_call(
        left_kernel,
        out_shape=sent,
        in_specs=[vmem, vmem],
        out_specs=vmem,
        compiler_params=params,
        cost_estimate=cost(10**8),
        name="left_sums",
    )(table, sums)
    after = lax.ppermute(left, "space", [((i + 1) % count, i) for i in range(count)])
    own = pl.pallas_call(
        own_kernel,
        out_shape=kept,
        in_specs=[vmem, vmem],
        out_specs=vmem,
        compiler_params=params,
        cost_estimate=cost(10**8),
        name="own_sums",
    )(table, sums)
    mean, anomalies = pl.pallas_call(
        members_kernel,
        out_shape=[jax.ShapeDtypeStruct((ncol, points), F32), jax.ShapeDtypeStruct((ncol * K, points), BF16)],
        in_specs=[vmem],
        out_specs=[vmem, vmem],
        compiler_params=params,
        cost_estimate=cost(10**8),
        name="member_means",
    )(ensemble[0])
    own = pl.pallas_call(
        before_kernel,
        out_shape=kept,
        in_specs=[vmem] * 2,
        out_specs=vmem,
        compiler_params=params,
        name="add_before",
    )(own, before)
    mixed = pl.pallas_call(
        after_kernel,
        out_shape=sent,
        in_specs=[vmem] * 2,
        out_specs=vmem,
        compiler_params=params,
        name="add_after",
    )(own, after)
    parts = lax.all_gather(mixed, "lag")
    out = pl.pallas_call(
        finish_kernel,
        out_shape=jax.ShapeDtypeStruct((ncol, K, points), BF16),
        in_specs=[vmem] * 3,
        out_specs=pl.BlockSpec(memory_space=pl.ANY),
        scratch_shapes=[VMEM((ncol, K, points), BF16), pltpu.SemaphoreType.DMA((U,))],
        compiler_params=params,
        name="transform_apply",
    )(parts, mean, anomalies)
    return out[None]


def solution(mesh):
    placed = (
        P("lag", "space", None, None),
        P(None, ("space", "lag")),
        P(("space", "lag")),
        P(("space", "lag")),
        P(("space", "lag")),
        P(("space", "lag")),
        P(),
    )
    return jax.shard_map(
        on_device,
        mesh=mesh,
        in_specs=placed,
        out_specs=P("lag", "space", None, None),
        check_vma=False,
    )
```

```python
import jax
import jax.numpy as jnp
from jax import lax
from jax.experimental import pallas as pl
from jax.experimental.pallas import tpu as pltpu
from jax.sharding import PartitionSpec as P

NS_ITERS = 4
K = 64
REACH = 32
U = 8
W = 2 * K
Q = 4
GRAM = U * K
HALF = GRAM // 2
SENT = HALF + 48
F32 = jnp.float32
BF16 = jnp.bfloat16
VMEM = pltpu.VMEM


def halves(x):
    high = x.astype(BF16)
    return high, (x - high.astype(F32)).astype(BF16)


def iota(shape, axis):
    return lax.broadcasted_iota(jnp.int32, shape, axis)


def encode(folded, bvec, mvec, diag):
    bhi, blo = halves(bvec)
    mhi, mlo = halves(mvec)
    rest = [x.astype(F32) for x in (bhi, blo, mhi, mlo)] + [diag, jnp.zeros_like(diag)]
    return folded.astype(BF16), jnp.concatenate(rest, axis=0).astype(BF16)


def decode(ref, at=()):
    whole = ref[at + (slice(0, HALF),)].astype(F32)
    rest = ref[at + (slice(HALF, SENT),)].astype(F32)
    return whole, rest[0:8] + rest[8:16], rest[16:24] + rest[24:32], rest[32:40]


def mix(sums_ref, taper_ref, side):
    lane = iota((1, W), 1)
    row, col = iota((K, W), 0), iota((K, W), 1) % K

    def at(distance):
        d = min(abs(distance), REACH - 1)
        return taper_ref[d : d + 1, :]

    def same(f):
        return at(2 * f)

    def crossed(f):
        return jnp.where(lane < K, at(2 * f + 1), at(2 * f - 1))

    out = [None] * U
    cross = {f: crossed(f) for f in range(1 - U + U * side, U + U * side)}
    for u in range(U):
        here = sums_ref[K * u : K * (u + 1), :]
        swapped = pltpu.roll(here, K, 1)
        for v in range(U):
            f = u - v + U * side
            term = here * same(f) + swapped * cross[f]
            out[v] = term if u == 0 else out[v] + term
    folded = jnp.concatenate([jnp.where(row <= col, out[v], out[v + U // 2]) for v in range(U // 2)], axis=0)
    sub = iota((U, W), 0)
    diag = jnp.zeros((U, W), F32)
    for v in range(U // 2):
        line = jnp.sum(jnp.where(row == col, out[v + U // 2], 0.0), axis=0, keepdims=True)
        diag = jnp.where(sub == v, line, diag)
    vectors = []
    for start in (GRAM, GRAM + U):
        here = sums_ref[start : start + U, :]
        swapped = pltpu.roll(here, K, 1)
        total = jnp.zeros((U, W), F32)
        for d in range(U):
            f, g = U * side - d, U * side - d + U
            turned, also = (pltpu.roll(x, d, 0) if d else x for x in (here, swapped))
            total = total + turned * jnp.where(sub >= d, same(f), same(g))
            total = total + also * jnp.where(sub >= d, crossed(f), crossed(g))
        vectors.append(total)
    return folded, vectors[0], vectors[1], diag


def store(out_ref, parts):
    folded, rest = encode(*parts)
    out_ref[0:HALF, :] = folded
    out_ref[HALF:SENT, :] = rest


def lanes_kernel(out_ref):
    out_ref[...] = iota(out_ref.shape, 1)


def obs_kernel(count_ref, taper_ref, lanes_ref, anom_ref, innov_ref, invv_ref, col_ref, sums_ref, table_ref, right_ref):
    slots = anom_ref.shape[1]
    for d in range(REACH):
        table_ref[d : d + 1, :] = jnp.full((1, W), taper_ref[d], F32)
    rinv = jnp.where(lanes_ref[0:1, :] < count_ref[0], invv_ref[...], 0.0)
    column = col_ref[...]
    outer, inner = column // Q, column % Q
    scaled = [jnp.where(outer == a, rinv, 0.0) for a in range(Q)]
    whole = anom_ref[...]
    mean = jnp.sum(whole, axis=0, keepdims=True) * (1.0 / K)
    anom = whole - mean
    left = [anom * scaled[a] for a in range(Q)]
    row = iota((16, slots), 0)
    rows = jnp.where(row < Q, innov_ref[...] * rinv, jnp.where(row < 2 * Q, mean * rinv, 0.0))
    left.append(jnp.where(row % Q == outer, rows, 0.0))
    lhi, llo = halves(jnp.concatenate(left, axis=0))
    rhi, rlo = halves(jnp.concatenate([jnp.where(inner == b, anom, 0.0) for b in range(Q)], axis=0))
    mhi, mlo = halves(jnp.where(iota((16, slots), 0) == inner, mean, 0.0))

    def dot(a, b):
        return lax.dot_general(a, b, (((1,), (1,)), ((), ())), preferred_element_type=F32)

    n = Q * K + 16
    both = dot(jnp.concatenate([lhi, llo], axis=0), rhi)
    sums = both[:n] + (both[n:] + dot(lhi, rlo))
    thi, tlo = lhi[Q * K :], llo[Q * K :]
    scalars = dot(thi, mhi) + (dot(thi, mlo) + dot(tlo, mhi))
    lane = iota((1, Q * K), 1) // K
    spread = jnp.zeros((8, Q * K), F32)
    for b in range(Q):
        spread = jnp.where(lane == b, scalars[:8, b : b + 1], spread)
    factor = jnp.where(iota((8, 1), 0) < Q, 1.0, 0.5)
    vectors = sums[Q * K : Q * K + 8] + spread * factor
    for a in range(Q):
        for i in range(2):
            u = 2 * a + i
            sums_ref[K * u : K * (u + 1), :] = sums[K * a : K * (a + 1), W * i : W * (i + 1)]
            sums_ref[GRAM + u : GRAM + u + 1, :] = vectors[a : a + 1, W * i : W * (i + 1)]
            sums_ref[GRAM + U + u : GRAM + U + u + 1, :] = vectors[Q + a : Q + a + 1, W * i : W * (i + 1)]
    store(right_ref, mix(sums_ref, table_ref, -1))


def left_kernel(taper_ref, sums_ref, left_ref):
    store(left_ref, mix(sums_ref, taper_ref, 1))


def put(out_ref, parts):
    folded, bvec, mvec, diag = parts
    out_ref[0:HALF, :] = folded
    out_ref[HALF : HALF + 8, :] = bvec
    out_ref[HALF + 8 : HALF + 16, :] = mvec
    out_ref[HALF + 16 : HALF + 24, :] = diag


def get(ref):
    return [ref[0:HALF, :]] + [ref[HALF + 8 * i : HALF + 8 * (i + 1), :] for i in range(3)]


def own_kernel(taper_ref, sums_ref, own_ref):
    put(own_ref, mix(sums_ref, taper_ref, 0))


def before_kernel(own_ref, before_ref, out_ref):
    put(out_ref, [x + y for x, y in zip(get(own_ref), decode(before_ref))])


def after_kernel(own_ref, after_ref, out_ref):
    store(out_ref, [x + y for x, y in zip(get(own_ref), decode(after_ref))])


def members_kernel(ens_ref, mean_ref, anom_ref):
    for c in range(ens_ref.shape[0]):
        members = ens_ref[c].astype(F32)
        mean = jnp.sum(members, axis=0, keepdims=True) * (1.0 / K)
        mean_ref[c : c + 1, :] = mean
        anom_ref[K * c : K * (c + 1), :] = (members - mean).astype(BF16)


def finish_kernel(parts_ref, mean_ref, anom_ref, out_ref, buf, sems):
    width = W
    groups = U
    n = W // K
    lane = iota((1, width), 1) // K
    diagonal = iota((width, width), 0) // K == iota((width, width), 1) // K
    eye = jnp.where(iota((K, width), 0) == iota((K, width), 1) % K, 1.0, 0.0)
    row, col = iota((K, W), 0), iota((K, W), 1) % K
    left_half = iota((K, W), 1) < K

    def spread(x):
        tall = jnp.concatenate([x] * n, axis=0)
        return jnp.where(diagonal, tall, jnp.zeros_like(tall))

    def dot(a, b):
        return jnp.dot(a, b, preferred_element_type=F32)

    def times(left, right):
        count = len(left)
        parts = [halves(x) for x in left]
        hi = [p[0] for p in parts]
        lo = [p[1] for p in parts]
        rhi, rlo = halves(right)
        first = dot(jnp.concatenate(hi + lo, axis=0), spread(rhi))
        second = dot(jnp.concatenate(hi, axis=0), spread(rlo))
        out = first[: count * K] + (first[count * K :] + second)
        return [out[i * K : (i + 1) * K] for i in range(count)]

    def lane_sums(x):
        out = jnp.zeros_like(x)
        for cc in range(n):
            out = jnp.where(lane == cc, jnp.sum(jnp.where(lane == cc, x, 0.0), axis=1, keepdims=True), out)
        return out

    folded, bvec, mvec, diag = decode(parts_ref, (0,))
    for lag in range(1, parts_ref.shape[0]):
        more = decode(parts_ref, (lag,))
        folded, bvec, mvec, diag = folded + more[0], bvec + more[1], mvec + more[2], diag + more[3]
    units = [None] * U
    for v in range(U // 2):
        here = folded[K * v : K * (v + 1)]
        if v % 2 == 0:
            square = jnp.transpose(folded[K * v : K * (v + 2)])
            upper, lower = square[:K], square[K:]
            turned = jnp.where(left_half, upper, pltpu.roll(lower, K, 1))
        else:
            turned = jnp.where(left_half, pltpu.roll(upper, K, 1), lower)
        units[v] = jnp.where(row <= col, here, turned)
        units[v + U // 2] = jnp.where(row == col, diag[v : v + 1], jnp.where(row > col, here, turned))
    bvec = [bvec[g : g + 1] for g in range(groups)]
    mvec = [mvec[g : g + 1] for g in range(groups)]
    parts = []
    for g in range(groups):
        line = eye * mvec[g]
        high, low = halves(line)
        parts += [high, low, (line - high.astype(F32) - low.astype(F32)).astype(BF16)]
    ones = jnp.where(diagonal, 1.0, 0.0).astype(BF16)
    across = dot(jnp.concatenate(parts, axis=0), ones)
    across = [sum(across[K * (3 * g + i) : K * (3 * g + i + 1)] for i in range(3)) for g in range(groups)]
    amat = [
        units[g] + mvec[g] + across[g] + (K - 1.0) * eye
        for g in range(groups)
    ]
    norms = jnp.concatenate([jnp.sum(a * a, axis=0, keepdims=True) for a in amat], axis=0)
    scale = jnp.sqrt(lane_sums(norms))
    scale = [scale[g : g + 1] for g in range(groups)]
    square = [times([a], a)[0] for a in amat]
    inverse = [1.0 / s for s in scale]
    zval = [1.5 * eye - (0.5 * i) * a for a, i in zip(amat, inverse)]
    yval = [(1.5 * i) * a - (0.5 * i * i) * q for a, i, q in zip(amat, inverse, square)]
    for step in range(1, NS_ITERS):
        prod = [times([z], y)[0] for z, y in zip(zval, yval)]
        mval = [1.5 * eye - 0.5 * p for p in prod]
        if step < NS_ITERS - 1:
            both = [times([y, z], m) for y, z, m in zip(yval, zval, mval)]
            yval, zval = [b[0] for b in both], [b[1] for b in both]
        else:
            zval = [times([z], m)[0] for z, m in zip(zval, mval)]
    weights = []
    for g in range(groups):
        inner = lane_sums(zval[g] * bvec[g])
        shift = jnp.sum(zval[g] * inner, axis=0, keepdims=True) * inverse[g]
        weights.append((zval[g] * jnp.sqrt((K - 1.0) * inverse[g]) + shift).astype(BF16))
    copies = []
    for g in range(groups):
        mixed = dot(spread(weights[g]), anom_ref[width * g : width * (g + 1), :])
        for cc in range(n):
            c = n * g + cc
            buf[c] = (mean_ref[c : c + 1, :] + mixed[K * cc : K * (cc + 1)]).astype(BF16)
        copies.append(pltpu.make_async_copy(buf.at[pl.ds(n * g, n)], out_ref.at[pl.ds(n * g, n)], sems.at[g]))
        copies[-1].start()
    for copy in copies:
        copy.wait()


def on_device(ensemble, obs_anomaly, innovation, inv_variance, obs_column, obs_count, taper):
    slots = obs_anomaly.shape[1]
    _, ncol, _, points = ensemble.shape
    vmem = pl.BlockSpec(memory_space=VMEM)
    smem = pl.BlockSpec(memory_space=pltpu.SMEM)
    params = pltpu.CompilerParams(vmem_limit_bytes=48 * 2**20)
    sent = jax.ShapeDtypeStruct((SENT, W), BF16)
    kept = jax.ShapeDtypeStruct((HALF + 24, W), F32)

    def cost(flops):
        return pl.CostEstimate(flops=flops, bytes_accessed=2**19, transcendentals=0)

    lanes = pl.pallas_call(
        lanes_kernel,
        out_shape=jax.ShapeDtypeStruct((8, slots), jnp.int32),
        out_specs=vmem,
        compiler_params=params,
        cost_estimate=cost(10**9),
        name="lane_numbers",
    )()
    sums, table, right = pl.pallas_call(
        obs_kernel,
        out_shape=[jax.ShapeDtypeStruct((GRAM + 2 * U, W), F32), jax.ShapeDtypeStruct((REACH, W), F32), sent],
        in_specs=[smem] * 2 + [vmem] * 5,
        out_specs=[vmem] * 3,
        compiler_params=params,
        name="obs_sums",
    )(obs_count, taper, lanes, obs_anomaly, innovation[None], inv_variance[None], obs_column[None])
    count = lax.axis_size("space")
    before = lax.ppermute(right, "space", [(i, (i + 1) % count) for i in range(count)])
    left = pl.pallas_call(
        left_kernel,
        out_shape=sent,
        in_specs=[vmem, vmem],
        out_specs=vmem,
        compiler_params=params,
        cost_estimate=cost(10**8),
        name="left_sums",
    )(table, sums)
    after = lax.ppermute(left, "space", [((i + 1) % count, i) for i in range(count)])
    own = pl.pallas_call(
        own_kernel,
        out_shape=kept,
        in_specs=[vmem, vmem],
        out_specs=vmem,
        compiler_params=params,
        cost_estimate=cost(10**8),
        name="own_sums",
    )(table, sums)
    mean, anomalies = pl.pallas_call(
        members_kernel,
        out_shape=[jax.ShapeDtypeStruct((ncol, points), F32), jax.ShapeDtypeStruct((ncol * K, points), BF16)],
        in_specs=[vmem],
        out_specs=[vmem, vmem],
        compiler_params=params,
        cost_estimate=cost(10**8),
        name="member_means",
    )(ensemble[0])
    own = pl.pallas_call(
        before_kernel,
        out_shape=kept,
        in_specs=[vmem] * 2,
        out_specs=vmem,
        compiler_params=params,
        name="add_before",
    )(own, before)
    mixed = pl.pallas_call(
        after_kernel,
        out_shape=sent,
        in_specs=[vmem] * 2,
        out_specs=vmem,
        compiler_params=params,
        name="add_after",
    )(own, after)
    parts = lax.all_gather(mixed, "lag")
    out = pl.pallas_call(
        finish_kernel,
        out_shape=jax.ShapeDtypeStruct((ncol, K, points), BF16),
        in_specs=[vmem] * 3,
        out_specs=pl.BlockSpec(memory_space=pl.ANY),
        scratch_shapes=[VMEM((ncol, K, points), BF16), pltpu.SemaphoreType.DMA((U,))],
        compiler_params=params,
        name="transform_apply",
    )(parts, mean, anomalies)
    return out[None]


def solution(mesh):
    placed = (
        P("lag", "space", None, None),
        P(None, ("space", "lag")),
        P(("space", "lag")),
        P(("space", "lag")),
        P(("space", "lag")),
        P(("space", "lag")),
        P(),
    )
    return jax.shard_map(
        on_device,
        mesh=mesh,
        in_specs=placed,
        out_specs=P("lag", "space", None, None),
        check_vma=False,
    )
```

```python
import jax
import jax.numpy as jnp
from jax import lax
from jax.experimental import pallas as pl
from jax.experimental.pallas import tpu as pltpu
from jax.sharding import PartitionSpec as P

NS_ITERS = 4
K = 64
REACH = 32
U = 8
W = 2 * K
Q = 4
GRAM = U * K
HALF = GRAM // 2
SENT = HALF + 48
F32 = jnp.float32
BF16 = jnp.bfloat16
VMEM = pltpu.VMEM


def halves(x):
    high = x.astype(BF16)
    return high, (x - high.astype(F32)).astype(BF16)


def iota(shape, axis):
    return lax.broadcasted_iota(jnp.int32, shape, axis)


def encode(folded, bvec, mvec, diag):
    bhi, blo = halves(bvec)
    mhi, mlo = halves(mvec)
    rest = [x.astype(F32) for x in (bhi, blo, mhi, mlo)] + [diag, jnp.zeros_like(diag)]
    return folded.astype(BF16), jnp.concatenate(rest, axis=0).astype(BF16)


def decode(ref, at=()):
    whole = ref[at + (slice(0, HALF),)].astype(F32)
    rest = ref[at + (slice(HALF, SENT),)].astype(F32)
    return whole, rest[0:8] + rest[8:16], rest[16:24] + rest[24:32], rest[32:40]


def mix(sums_ref, taper_ref, side):
    lane = iota((1, W), 1)
    row, col = iota((K, W), 0), iota((K, W), 1) % K

    def at(distance):
        d = min(abs(distance), REACH - 1)
        return taper_ref[d : d + 1, :]

    def same(f):
        return at(2 * f)

    def crossed(f):
        return jnp.where(lane < K, at(2 * f + 1), at(2 * f - 1))

    out = [None] * U
    cross = {f: crossed(f) for f in range(1 - U + U * side, U + U * side)}
    for u in range(U):
        here = sums_ref[K * u : K * (u + 1), :]
        swapped = pltpu.roll(here, K, 1)
        for v in range(U):
            f = u - v + U * side
            term = here * same(f) + swapped * cross[f]
            out[v] = term if u == 0 else out[v] + term
    folded = jnp.concatenate([jnp.where(row <= col, out[v], out[v + U // 2]) for v in range(U // 2)], axis=0)
    sub = iota((U, W), 0)
    diag = jnp.zeros((U, W), F32)
    for v in range(U // 2):
        line = jnp.sum(jnp.where(row == col, out[v + U // 2], 0.0), axis=0, keepdims=True)
        diag = jnp.where(sub == v, line, diag)
    vectors = []
    for start in (GRAM, GRAM + U):
        here = sums_ref[start : start + U, :]
        swapped = pltpu.roll(here, K, 1)
        total = jnp.zeros((U, W), F32)
        for d in range(U):
            f, g = U * side - d, U * side - d + U
            turned, also = (pltpu.roll(x, d, 0) if d else x for x in (here, swapped))
            total = total + turned * jnp.where(sub >= d, same(f), same(g))
            total = total + also * jnp.where(sub >= d, crossed(f), crossed(g))
        vectors.append(total)
    return folded, vectors[0], vectors[1], diag


def store(out_ref, parts):
    folded, rest = encode(*parts)
    out_ref[0:HALF, :] = folded
    out_ref[HALF:SENT, :] = rest


def lanes_kernel(out_ref):
    out_ref[...] = iota(out_ref.shape, 1)


def obs_kernel(count_ref, taper_ref, lanes_ref, anom_ref, innov_ref, invv_ref, col_ref, sums_ref, table_ref, right_ref):
    slots = anom_ref.shape[1]
    square = (REACH, REACH)
    entries = jnp.where(iota(square, 0) == iota(square, 1), taper_ref[...], 0.0)
    table_ref[...] = jnp.broadcast_to(jnp.sum(entries, axis=1, keepdims=True), (REACH, W))
    rinv = jnp.where(lanes_ref[0:1, :] < count_ref[0], invv_ref[...], 0.0)
    column = col_ref[...]
    outer, inner = column // Q, column % Q
    scaled = [jnp.where(outer == a, rinv, 0.0) for a in range(Q)]
    whole = anom_ref[...]
    mean = jnp.sum(whole, axis=0, keepdims=True) * (1.0 / K)
    anom = whole - mean
    left = [anom * scaled[a] for a in range(Q)]
    row = iota((16, slots), 0)
    rows = jnp.where(row < Q, innov_ref[...] * rinv, jnp.where(row < 2 * Q, mean * rinv, 0.0))
    left.append(jnp.where(row % Q == outer, rows, 0.0))
    lhi, llo = halves(jnp.concatenate(left, axis=0))
    rhi, rlo = halves(jnp.concatenate([jnp.where(inner == b, anom, 0.0) for b in range(Q)], axis=0))
    mhi, mlo = halves(jnp.where(iota((16, slots), 0) == inner, mean, 0.0))

    def dot(a, b):
        return lax.dot_general(a, b, (((1,), (1,)), ((), ())), preferred_element_type=F32)

    n = Q * K + 16
    both = dot(jnp.concatenate([lhi, llo], axis=0), rhi)
    sums = both[:n] + (both[n:] + dot(lhi, rlo))
    thi, tlo = lhi[Q * K :], llo[Q * K :]
    scalars = dot(thi, mhi) + (dot(thi, mlo) + dot(tlo, mhi))
    lane = iota((1, Q * K), 1) // K
    spread = jnp.zeros((8, Q * K), F32)
    for b in range(Q):
        spread = jnp.where(lane == b, scalars[:8, b : b + 1], spread)
    factor = jnp.where(iota((8, 1), 0) < Q, 1.0, 0.5)
    vectors = sums[Q * K : Q * K + 8] + spread * factor
    for a in range(Q):
        for i in range(2):
            u = 2 * a + i
            sums_ref[K * u : K * (u + 1), :] = sums[K * a : K * (a + 1), W * i : W * (i + 1)]
            sums_ref[GRAM + u : GRAM + u + 1, :] = vectors[a : a + 1, W * i : W * (i + 1)]
            sums_ref[GRAM + U + u : GRAM + U + u + 1, :] = vectors[Q + a : Q + a + 1, W * i : W * (i + 1)]
    store(right_ref, mix(sums_ref, table_ref, -1))


def left_kernel(taper_ref, sums_ref, left_ref):
    store(left_ref, mix(sums_ref, taper_ref, 1))


def put(out_ref, parts):
    folded, bvec, mvec, diag = parts
    out_ref[0:HALF, :] = folded
    out_ref[HALF : HALF + 8, :] = bvec
    out_ref[HALF + 8 : HALF + 16, :] = mvec
    out_ref[HALF + 16 : HALF + 24, :] = diag


def get(ref):
    return [ref[0:HALF, :]] + [ref[HALF + 8 * i : HALF + 8 * (i + 1), :] for i in range(3)]


def own_kernel(taper_ref, sums_ref, own_ref):
    put(own_ref, mix(sums_ref, taper_ref, 0))


def before_kernel(own_ref, before_ref, out_ref):
    put(out_ref, [x + y for x, y in zip(get(own_ref), decode(before_ref))])


def after_kernel(own_ref, after_ref, out_ref):
    store(out_ref, [x + y for x, y in zip(get(own_ref), decode(after_ref))])


def members_kernel(ens_ref, mean_ref, anom_ref):
    for c in range(ens_ref.shape[0]):
        members = ens_ref[c].astype(F32)
        mean = jnp.sum(members, axis=0, keepdims=True) * (1.0 / K)
        mean_ref[c : c + 1, :] = mean
        anom_ref[K * c : K * (c + 1), :] = (members - mean).astype(BF16)


def finish_kernel(parts_ref, mean_ref, anom_ref, out_ref, buf, sems):
    width = W
    groups = U
    n = W // K
    lane = iota((1, width), 1) // K
    diagonal = iota((width, width), 0) // K == iota((width, width), 1) // K
    eye = jnp.where(iota((K, width), 0) == iota((K, width), 1) % K, 1.0, 0.0)
    row, col = iota((K, W), 0), iota((K, W), 1) % K
    left_half = iota((K, W), 1) < K

    def spread(x):
        tall = jnp.concatenate([x] * n, axis=0)
        return jnp.where(diagonal, tall, jnp.zeros_like(tall))

    def dot(a, b):
        return jnp.dot(a, b, preferred_element_type=F32)

    def times(left, right):
        count = len(left)
        parts = [halves(x) for x in left]
        hi = [p[0] for p in parts]
        lo = [p[1] for p in parts]
        rhi, rlo = halves(right)
        first = dot(jnp.concatenate(hi + lo, axis=0), spread(rhi))
        second = dot(jnp.concatenate(hi, axis=0), spread(rlo))
        out = first[: count * K] + (first[count * K :] + second)
        return [out[i * K : (i + 1) * K] for i in range(count)]

    def lane_sums(x):
        out = jnp.zeros_like(x)
        for cc in range(n):
            out = jnp.where(lane == cc, jnp.sum(jnp.where(lane == cc, x, 0.0), axis=1, keepdims=True), out)
        return out

    folded, bvec, mvec, diag = decode(parts_ref, (0,))
    for lag in range(1, parts_ref.shape[0]):
        more = decode(parts_ref, (lag,))
        folded, bvec, mvec, diag = folded + more[0], bvec + more[1], mvec + more[2], diag + more[3]
    units = [None] * U
    for v in range(U // 2):
        here = folded[K * v : K * (v + 1)]
        if v % 2 == 0:
            square = jnp.transpose(folded[K * v : K * (v + 2)])
            upper, lower = square[:K], square[K:]
            turned = jnp.where(left_half, upper, pltpu.roll(lower, K, 1))
        else:
            turned = jnp.where(left_half, pltpu.roll(upper, K, 1), lower)
        units[v] = jnp.where(row <= col, here, turned)
        units[v + U // 2] = jnp.where(row == col, diag[v : v + 1], jnp.where(row > col, here, turned))
    bvec = [bvec[g : g + 1] for g in range(groups)]
    mvec = [mvec[g : g + 1] for g in range(groups)]
    parts = []
    for g in range(groups):
        line = eye * mvec[g]
        high, low = halves(line)
        parts += [high, low, (line - high.astype(F32) - low.astype(F32)).astype(BF16)]
    ones = jnp.where(diagonal, 1.0, 0.0).astype(BF16)
    across = dot(jnp.concatenate(parts, axis=0), ones)
    across = [sum(across[K * (3 * g + i) : K * (3 * g + i + 1)] for i in range(3)) for g in range(groups)]
    amat = [
        units[g] + mvec[g] + across[g] + (K - 1.0) * eye
        for g in range(groups)
    ]
    norms = jnp.concatenate([jnp.sum(a * a, axis=0, keepdims=True) for a in amat], axis=0)
    scale = jnp.sqrt(lane_sums(norms))
    scale = [scale[g : g + 1] for g in range(groups)]
    square = [times([a], a)[0] for a in amat]
    inverse = [1.0 / s for s in scale]
    zval = [1.5 * eye - (0.5 * i) * a for a, i in zip(amat, inverse)]
    yval = [(1.5 * i) * a - (0.5 * i * i) * q for a, i, q in zip(amat, inverse, square)]
    for step in range(1, NS_ITERS):
        prod = [times([z], y)[0] for z, y in zip(zval, yval)]
        mval = [1.5 * eye - 0.5 * p for p in prod]
        if step < NS_ITERS - 1:
            both = [times([y, z], m) for y, z, m in zip(yval, zval, mval)]
            yval, zval = [b[0] for b in both], [b[1] for b in both]
        else:
            zval = [times([z], m)[0] for z, m in zip(zval, mval)]
    weights = []
    for g in range(groups):
        inner = lane_sums(zval[g] * bvec[g])
        shift = jnp.sum(zval[g] * inner, axis=0, keepdims=True) * inverse[g]
        weights.append((zval[g] * jnp.sqrt((K - 1.0) * inverse[g]) + shift).astype(BF16))
    copies = []
    for g in range(groups):
        mixed = dot(spread(weights[g]), anom_ref[width * g : width * (g + 1), :])
        for cc in range(n):
            c = n * g + cc
            buf[c] = (mean_ref[c : c + 1, :] + mixed[K * cc : K * (cc + 1)]).astype(BF16)
        copies.append(pltpu.make_async_copy(buf.at[pl.ds(n * g, n)], out_ref.at[pl.ds(n * g, n)], sems.at[g]))
        copies[-1].start()
    for copy in copies:
        copy.wait()


def on_device(ensemble, obs_anomaly, innovation, inv_variance, obs_column, obs_count, taper):
    slots = obs_anomaly.shape[1]
    _, ncol, _, points = ensemble.shape
    vmem = pl.BlockSpec(memory_space=VMEM)
    smem = pl.BlockSpec(memory_space=pltpu.SMEM)
    params = pltpu.CompilerParams(vmem_limit_bytes=48 * 2**20)
    sent = jax.ShapeDtypeStruct((SENT, W), BF16)
    kept = jax.ShapeDtypeStruct((HALF + 24, W), F32)

    def cost(flops):
        return pl.CostEstimate(flops=flops, bytes_accessed=2**19, transcendentals=0)

    lanes = pl.pallas_call(
        lanes_kernel,
        out_shape=jax.ShapeDtypeStruct((8, slots), jnp.int32),
        out_specs=vmem,
        compiler_params=params,
        cost_estimate=cost(10**9),
        name="lane_numbers",
    )()
    sums, table, right = pl.pallas_call(
        obs_kernel,
        out_shape=[jax.ShapeDtypeStruct((GRAM + 2 * U, W), F32), jax.ShapeDtypeStruct((REACH, W), F32), sent],
        in_specs=[smem] + [vmem] * 6,
        out_specs=[vmem] * 3,
        compiler_params=params,
        name="obs_sums",
    )(obs_count, taper[None], lanes, obs_anomaly, innovation[None], inv_variance[None], obs_column[None])
    count = lax.axis_size("space")
    before = lax.ppermute(right, "space", [(i, (i + 1) % count) for i in range(count)])
    left = pl.pallas_call(
        left_kernel,
        out_shape=sent,
        in_specs=[vmem, vmem],
        out_specs=vmem,
        compiler_params=params,
        cost_estimate=cost(10**8),
        name="left_sums",
    )(table, sums)
    after = lax.ppermute(left, "space", [((i + 1) % count, i) for i in range(count)])
    own = pl.pallas_call(
        own_kernel,
        out_shape=kept,
        in_specs=[vmem, vmem],
        out_specs=vmem,
        compiler_params=params,
        cost_estimate=cost(10**8),
        name="own_sums",
    )(table, sums)
    mean, anomalies = pl.pallas_call(
        members_kernel,
        out_shape=[jax.ShapeDtypeStruct((ncol, points), F32), jax.ShapeDtypeStruct((ncol * K, points), BF16)],
        in_specs=[vmem],
        out_specs=[vmem, vmem],
        compiler_params=params,
        cost_estimate=cost(10**8),
        name="member_means",
    )(ensemble[0])
    own = pl.pallas_call(
        before_kernel,
        out_shape=kept,
        in_specs=[vmem] * 2,
        out_specs=vmem,
        compiler_params=params,
        name="add_before",
    )(own, before)
    mixed = pl.pallas_call(
        after_kernel,
        out_shape=sent,
        in_specs=[vmem] * 2,
        out_specs=vmem,
        compiler_params=params,
        name="add_after",
    )(own, after)
    parts = lax.all_gather(mixed, "lag")
    out = pl.pallas_call(
        finish_kernel,
        out_shape=jax.ShapeDtypeStruct((ncol, K, points), BF16),
        in_specs=[vmem] * 3,
        out_specs=pl.BlockSpec(memory_space=pl.ANY),
        scratch_shapes=[VMEM((ncol, K, points), BF16), pltpu.SemaphoreType.DMA((U,))],
        compiler_params=params,
        name="transform_apply",
    )(parts, mean, anomalies)
    return out[None]


def solution(mesh):
    placed = (
        P("lag", "space", None, None),
        P(None, ("space", "lag")),
        P(("space", "lag")),
        P(("space", "lag")),
        P(("space", "lag")),
        P(("space", "lag")),
        P(),
    )
    return jax.shard_map(
        on_device,
        mesh=mesh,
        in_specs=placed,
        out_specs=P("lag", "space", None, None),
        check_vma=False,
    )
```

```python
import jax
import jax.numpy as jnp
from jax import lax
from jax.experimental import pallas as pl
from jax.experimental.pallas import tpu as pltpu
from jax.sharding import PartitionSpec as P

TWO_STEPS = (2.25, -2.4375, 1.6875, -0.5625, 0.0625)
K = 64
REACH = 32
U = 8
W = 2 * K
Q = 4
GRAM = U * K
HALF = GRAM // 2
SENT = HALF + 48
F32 = jnp.float32
BF16 = jnp.bfloat16
VMEM = pltpu.VMEM


def halves(x):
    high = x.astype(BF16)
    return high, (x - high.astype(F32)).astype(BF16)


def iota(shape, axis):
    return lax.broadcasted_iota(jnp.int32, shape, axis)


def encode(folded, bvec, mvec, diag):
    bhi, blo = halves(bvec)
    mhi, mlo = halves(mvec)
    rest = [x.astype(F32) for x in (bhi, blo, mhi, mlo)] + [diag, jnp.zeros_like(diag)]
    return folded.astype(BF16), jnp.concatenate(rest, axis=0).astype(BF16)


def decode(ref, at=()):
    whole = ref[at + (slice(0, HALF),)].astype(F32)
    rest = ref[at + (slice(HALF, SENT),)].astype(F32)
    return whole, rest[0:8] + rest[8:16], rest[16:24] + rest[24:32], rest[32:40]


def mix(sums_ref, taper_ref, side):
    lane = iota((1, W), 1)
    row, col = iota((K, W), 0), iota((K, W), 1) % K

    def at(distance):
        d = min(abs(distance), REACH - 1)
        return taper_ref[d : d + 1, :]

    def same(f):
        return at(2 * f)

    def crossed(f):
        return jnp.where(lane < K, at(2 * f + 1), at(2 * f - 1))

    upper = row <= col
    half = U // 2
    straight, cross = {}, {}
    for f in range(1 - half + U * side, U + U * side):
        straight[f] = jnp.where(upper, same(f), same(f - half))
        cross[f] = jnp.where(upper, crossed(f), crossed(f - half))
    out = [None] * half
    for u in range(U):
        here = sums_ref[K * u : K * (u + 1), :]
        swapped = pltpu.roll(here, K, 1)
        for v in range(half):
            f = u - v + U * side
            term = here * straight[f] + swapped * cross[f]
            out[v] = term if u == 0 else out[v] + term
    folded = jnp.concatenate(out, axis=0)
    sub = iota((U, W), 0)
    vectors = []
    for start in (GRAM, GRAM + U, GRAM + 2 * U):
        here = sums_ref[start : start + U, :]
        swapped = pltpu.roll(here, K, 1)
        total = jnp.zeros((U, W), F32)
        for d in range(U):
            f, g = U * side - d, U * side - d + U
            turned, also = (pltpu.roll(x, d, 0) if d else x for x in (here, swapped))
            total = total + turned * jnp.where(sub >= d, same(f), same(g))
            total = total + also * jnp.where(sub >= d, crossed(f), crossed(g))
        vectors.append(total)
    return folded, vectors[0], vectors[1], jnp.where(sub < half, pltpu.roll(vectors[2], half, 0), 0.0)


def store(out_ref, parts):
    folded, rest = encode(*parts)
    out_ref[0:HALF, :] = folded
    out_ref[HALF:SENT, :] = rest


def lanes_kernel(out_ref):
    out_ref[...] = iota(out_ref.shape, 1)


def obs_kernel(count_ref, taper_ref, lanes_ref, anom_ref, innov_ref, invv_ref, col_ref, sums_ref, table_ref, right_ref):
    slots = anom_ref.shape[1]
    square = (REACH, REACH)
    entries = jnp.where(iota(square, 0) == iota(square, 1), taper_ref[...], 0.0)
    table_ref[...] = jnp.broadcast_to(jnp.sum(entries, axis=1, keepdims=True), (REACH, W))
    rinv = jnp.where(lanes_ref[0:1, :] < count_ref[0], invv_ref[...], 0.0)
    column = col_ref[...]
    outer, inner = column // Q, column % Q
    scaled = [jnp.where(outer == a, rinv, 0.0) for a in range(Q)]
    whole = anom_ref[...]
    mean = jnp.sum(whole, axis=0, keepdims=True) * (1.0 / K)
    anom = whole - mean
    left = [anom * scaled[a] for a in range(Q)]
    row = iota((16, slots), 0)
    rows = jnp.where(row < Q, innov_ref[...] * rinv, jnp.where(row < 2 * Q, mean * rinv, 0.0))
    left.append(jnp.where(row % Q == outer, rows, 0.0))
    lhi, llo = halves(jnp.concatenate(left, axis=0))
    rhi, rlo = halves(jnp.concatenate([jnp.where(inner == b, anom, 0.0) for b in range(Q)], axis=0))

    def dot(a, b):
        return lax.dot_general(a, b, (((1,), (1,)), ((), ())), preferred_element_type=F32)

    n = Q * K + 16
    both = dot(jnp.concatenate([lhi, llo], axis=0), rhi)
    sums = both[:n] + (both[n:] + dot(lhi, rlo))
    lane = iota((1, Q * K), 1) // K
    spread = jnp.zeros((8, Q * K), F32)
    product = left[Q][:8] * mean
    for b in range(Q):
        spread = jnp.where(lane == b, jnp.sum(jnp.where(inner == b, product, 0.0), axis=1, keepdims=True), spread)
    factor = jnp.where(iota((8, 1), 0) < Q, 1.0, 0.5)
    vectors = sums[Q * K : Q * K + 8] + spread * factor
    on = iota((K, W), 0) == iota((K, W), 1) % K
    for a in range(Q):
        for i in range(2):
            u = 2 * a + i
            here = sums[K * a : K * (a + 1), W * i : W * (i + 1)]
            sums_ref[K * u : K * (u + 1), :] = here
            sums_ref[GRAM + 2 * U + u : GRAM + 2 * U + u + 1, :] = jnp.sum(jnp.where(on, here, 0.0), axis=0, keepdims=True)
            sums_ref[GRAM + u : GRAM + u + 1, :] = vectors[a : a + 1, W * i : W * (i + 1)]
            sums_ref[GRAM + U + u : GRAM + U + u + 1, :] = vectors[Q + a : Q + a + 1, W * i : W * (i + 1)]
    store(right_ref, mix(sums_ref, table_ref, -1))


def left_kernel(taper_ref, sums_ref, left_ref):
    store(left_ref, mix(sums_ref, taper_ref, 1))


def put(out_ref, parts):
    folded, bvec, mvec, diag = parts
    out_ref[0:HALF, :] = folded
    out_ref[HALF : HALF + 8, :] = bvec
    out_ref[HALF + 8 : HALF + 16, :] = mvec
    out_ref[HALF + 16 : HALF + 24, :] = diag


def get(ref):
    return [ref[0:HALF, :]] + [ref[HALF + 8 * i : HALF + 8 * (i + 1), :] for i in range(3)]


def own_kernel(taper_ref, sums_ref, own_ref):
    put(own_ref, mix(sums_ref, taper_ref, 0))


def before_kernel(own_ref, before_ref, out_ref):
    put(out_ref, [x + y for x, y in zip(get(own_ref), decode(before_ref))])


def after_kernel(own_ref, after_ref, out_ref):
    store(out_ref, [x + y for x, y in zip(get(own_ref), decode(after_ref))])


def members_kernel(ens_ref, mean_ref, anom_ref):
    for c in range(ens_ref.shape[0]):
        members = ens_ref[c].astype(F32)
        mean = jnp.sum(members, axis=0, keepdims=True) * (1.0 / K)
        mean_ref[c : c + 1, :] = mean
        anom_ref[K * c : K * (c + 1), :] = (members - mean).astype(BF16)


def finish_kernel(parts_ref, mean_ref, anom_ref, out_ref, buf, sems):
    width = W
    groups = U
    n = W // K
    lane = iota((1, width), 1) // K
    diagonal = iota((width, width), 0) // K == iota((width, width), 1) // K
    eye = jnp.where(iota((K, width), 0) == iota((K, width), 1) % K, 1.0, 0.0)
    row, col = iota((K, W), 0), iota((K, W), 1) % K
    left_half = iota((K, W), 1) < K

    def spread(x):
        tall = jnp.concatenate([x] * n, axis=0)
        return jnp.where(diagonal, tall, jnp.zeros_like(tall))

    def dot(a, b):
        return jnp.dot(a, b, preferred_element_type=F32)

    def times(left, right):
        count = len(left)
        parts = [halves(x) for x in left]
        hi = [p[0] for p in parts]
        lo = [p[1] for p in parts]
        rhi, rlo = halves(right)
        first = dot(jnp.concatenate(hi + lo, axis=0), spread(rhi))
        second = dot(jnp.concatenate(hi, axis=0), spread(rlo))
        out = first[: count * K] + (first[count * K :] + second)
        return [out[i * K : (i + 1) * K] for i in range(count)]

    def lane_sums(x):
        out = jnp.zeros_like(x)
        for cc in range(n):
            out = jnp.where(lane == cc, jnp.sum(jnp.where(lane == cc, x, 0.0), axis=1, keepdims=True), out)
        return out

    folded, bvec, mvec, diag = decode(parts_ref, (0,))
    for lag in range(1, parts_ref.shape[0]):
        more = decode(parts_ref, (lag,))
        folded, bvec, mvec, diag = folded + more[0], bvec + more[1], mvec + more[2], diag + more[3]
    units = [None] * U
    for v in range(U // 2):
        here = folded[K * v : K * (v + 1)]
        if v % 2 == 0:
            square = jnp.transpose(folded[K * v : K * (v + 2)])
            upper, lower = square[:K], square[K:]
            turned = jnp.where(left_half, upper, pltpu.roll(lower, K, 1))
        else:
            turned = jnp.where(left_half, pltpu.roll(upper, K, 1), lower)
        units[v] = jnp.where(row <= col, here, turned)
        units[v + U // 2] = jnp.where(row == col, diag[v : v + 1], jnp.where(row > col, here, turned))
    bvec = [bvec[g : g + 1] for g in range(groups)]
    mvec = [mvec[g : g + 1] for g in range(groups)]
    parts = []
    for g in range(groups):
        line = eye * mvec[g]
        high, low = halves(line)
        parts += [high, low, (line - high.astype(F32) - low.astype(F32)).astype(BF16)]
    ones = jnp.where(diagonal, 1.0, 0.0).astype(BF16)
    across = dot(jnp.concatenate(parts, axis=0), ones)
    across = [sum(across[K * (3 * g + i) : K * (3 * g + i + 1)] for i in range(3)) for g in range(groups)]
    amat = [
        units[g] + mvec[g] + across[g] + (K - 1.0) * eye
        for g in range(groups)
    ]
    norms = jnp.concatenate([jnp.sum(a * a, axis=0, keepdims=True) for a in amat], axis=0)
    scale = jnp.sqrt(lane_sums(norms))
    scale = [scale[g : g + 1] for g in range(groups)]
    square = [times([a], a)[0] for a in amat]
    inverse = [1.0 / s for s in scale]
    one, two, three, four, five = TWO_STEPS
    x1 = [i * a for a, i in zip(amat, inverse)]
    x2 = [(i * i) * q for q, i in zip(square, inverse)]
    more = [times([p, q], q) for p, q in zip(x1, x2)]
    zval = [one * eye + two * p + three * q + (four * m[0] + five * m[1]) for p, q, m in zip(x1, x2, more)]
    more = [times([p, z], z) for p, z in zip(x1, zval)]
    more = [times([z, m[1]], m[0]) for z, m in zip(zval, more)]
    third = [times([m[0], m[1]], m[0]) for m in more]
    last = [times([four * m[1] + five * t[1]], t[0])[0] for m, t in zip(more, third)]
    zval = [one * z + two * m[1] + three * t[1] + y for z, m, t, y in zip(zval, more, third, last)]
    weights = []
    for g in range(groups):
        inner = lane_sums(zval[g] * bvec[g])
        shift = jnp.sum(zval[g] * inner, axis=0, keepdims=True) * inverse[g]
        weights.append((zval[g] * jnp.sqrt((K - 1.0) * inverse[g]) + shift).astype(BF16))
    copies = []
    for g in range(groups):
        mixed = dot(spread(weights[g]), anom_ref[width * g : width * (g + 1), :])
        for cc in range(n):
            c = n * g + cc
            buf[c] = (mean_ref[c : c + 1, :] + mixed[K * cc : K * (cc + 1)]).astype(BF16)
        copies.append(pltpu.make_async_copy(buf.at[pl.ds(n * g, n)], out_ref.at[pl.ds(n * g, n)], sems.at[g]))
        copies[-1].start()
    for copy in copies:
        copy.wait()


def on_device(ensemble, obs_anomaly, innovation, inv_variance, obs_column, obs_count, taper):
    slots = obs_anomaly.shape[1]
    _, ncol, _, points = ensemble.shape
    vmem = pl.BlockSpec(memory_space=VMEM)
    smem = pl.BlockSpec(memory_space=pltpu.SMEM)
    params = pltpu.CompilerParams(vmem_limit_bytes=48 * 2**20)
    sent = jax.ShapeDtypeStruct((SENT, W), BF16)
    kept = jax.ShapeDtypeStruct((HALF + 24, W), F32)

    def cost(flops):
        return pl.CostEstimate(flops=flops, bytes_accessed=2**19, transcendentals=0)

    lanes = pl.pallas_call(
        lanes_kernel,
        out_shape=jax.ShapeDtypeStruct((8, slots), jnp.int32),
        out_specs=vmem,
        compiler_params=params,
        cost_estimate=cost(10**9),
        name="lane_numbers",
    )()
    sums, table, right = pl.pallas_call(
        obs_kernel,
        out_shape=[jax.ShapeDtypeStruct((GRAM + 3 * U, W), F32), jax.ShapeDtypeStruct((REACH, W), F32), sent],
        in_specs=[smem] + [vmem] * 6,
        out_specs=[vmem] * 3,
        compiler_params=params,
        name="obs_sums",
    )(obs_count, taper[None], lanes, obs_anomaly, innovation[None], inv_variance[None], obs_column[None])
    count = lax.axis_size("space")
    before = lax.ppermute(right, "space", [(i, (i + 1) % count) for i in range(count)])
    left = pl.pallas_call(
        left_kernel,
        out_shape=sent,
        in_specs=[vmem, vmem],
        out_specs=vmem,
        compiler_params=params,
        cost_estimate=cost(10**8),
        name="left_sums",
    )(table, sums)
    after = lax.ppermute(left, "space", [((i + 1) % count, i) for i in range(count)])
    own = pl.pallas_call(
        own_kernel,
        out_shape=kept,
        in_specs=[vmem, vmem],
        out_specs=vmem,
        compiler_params=params,
        cost_estimate=cost(10**8),
        name="own_sums",
    )(table, sums)
    mean, anomalies = pl.pallas_call(
        members_kernel,
        out_shape=[jax.ShapeDtypeStruct((ncol, points), F32), jax.ShapeDtypeStruct((ncol * K, points), BF16)],
        in_specs=[vmem],
        out_specs=[vmem, vmem],
        compiler_params=params,
        cost_estimate=cost(10**8),
        name="member_means",
    )(ensemble[0])
    own = pl.pallas_call(
        before_kernel,
        out_shape=kept,
        in_specs=[vmem] * 2,
        out_specs=vmem,
        compiler_params=params,
        name="add_before",
    )(own, before)
    mixed = pl.pallas_call(
        after_kernel,
        out_shape=sent,
        in_specs=[vmem] * 2,
        out_specs=vmem,
        compiler_params=params,
        name="add_after",
    )(own, after)
    parts = lax.all_gather(mixed, "lag")
    out = pl.pallas_call(
        finish_kernel,
        out_shape=jax.ShapeDtypeStruct((ncol, K, points), BF16),
        in_specs=[vmem] * 3,
        out_specs=pl.BlockSpec(memory_space=pl.ANY),
        scratch_shapes=[VMEM((ncol, K, points), BF16), pltpu.SemaphoreType.DMA((U,))],
        compiler_params=params,
        name="transform_apply",
    )(parts, mean, anomalies)
    return out[None]


def solution(mesh):
    placed = (
        P("lag", "space", None, None),
        P(None, ("space", "lag")),
        P(("space", "lag")),
        P(("space", "lag")),
        P(("space", "lag")),
        P(("space", "lag")),
        P(),
    )
    return jax.shard_map(
        on_device,
        mesh=mesh,
        in_specs=placed,
        out_specs=P("lag", "space", None, None),
        check_vma=False,
    )
```

```python
import jax
import jax.numpy as jnp
from jax import lax
from jax.experimental import pallas as pl
from jax.experimental.pallas import tpu as pltpu
from jax.sharding import PartitionSpec as P

TWO_STEPS = (2.25, -2.4375, 1.6875, -0.5625, 0.0625)
K = 64
REACH = 32
U = 8
W = 2 * K
Q = 4
GRAM = U * K
HALF = GRAM // 2
SENT = HALF + 40
F32 = jnp.float32
BF16 = jnp.bfloat16
VMEM = pltpu.VMEM


def halves(x):
    high = x.astype(BF16)
    return high, (x - high.astype(F32)).astype(BF16)


def iota(shape, axis):
    return lax.broadcasted_iota(jnp.int32, shape, axis)


def encode(folded, bvec, mvec, diag):
    bhi, blo = halves(bvec)
    mhi, mlo = halves(mvec)
    rest = [x.astype(F32) for x in (bhi, blo, mhi, mlo)]
    return jnp.concatenate([folded, *rest, diag], axis=0).astype(BF16)


def decode(sent):
    whole = sent.astype(F32)
    bhi, blo, mhi, mlo, diag = (whole[HALF + 8 * i : HALF + 8 * (i + 1)] for i in range(5))
    return whole[:HALF], bhi + blo, mhi + mlo, diag


def mix(sums_ref, taper_ref, side):
    lane = iota((1, W), 1)
    row, col = iota((K, W), 0), iota((K, W), 1) % K

    def at(distance):
        d = min(abs(distance), REACH - 1)
        return taper_ref[d : d + 1, :]

    def same(f):
        return at(2 * f)

    def crossed(f):
        return jnp.where(lane < K, at(2 * f + 1), at(2 * f - 1))

    upper = row <= col
    half = U // 2
    straight, cross = {}, {}
    for f in range(1 - half + U * side, U + U * side):
        straight[f] = jnp.where(upper, same(f), same(f - half))
        cross[f] = jnp.where(upper, crossed(f), crossed(f - half))
    out = [None] * half
    for u in range(U):
        here = sums_ref[K * u : K * (u + 1), :]
        swapped = pltpu.roll(here, K, 1)
        for v in range(half):
            f = u - v + U * side
            term = here * straight[f] + swapped * cross[f]
            out[v] = term if u == 0 else out[v] + term
    folded = jnp.concatenate(out, axis=0)
    sub = iota((U, W), 0)
    vectors = []
    for start in (GRAM, GRAM + U, GRAM + 2 * U):
        here = sums_ref[start : start + U, :]
        swapped = pltpu.roll(here, K, 1)
        total = jnp.zeros((U, W), F32)
        for d in range(U):
            f, g = U * side - d, U * side - d + U
            turned, also = (pltpu.roll(x, d, 0) if d else x for x in (here, swapped))
            total = total + turned * jnp.where(sub >= d, same(f), same(g))
            total = total + also * jnp.where(sub >= d, crossed(f), crossed(g))
        vectors.append(total)
    return folded, vectors[0], vectors[1], jnp.where(sub < half, pltpu.roll(vectors[2], half, 0), 0.0)


def store(out_ref, parts):
    out_ref[...] = encode(*parts)


def lanes_kernel(out_ref):
    out_ref[...] = iota(out_ref.shape, 1)


def obs_kernel(count_ref, taper_ref, lanes_ref, anom_ref, innov_ref, invv_ref, col_ref, sums_ref, table_ref, right_ref):
    slots = anom_ref.shape[1]
    square = (REACH, REACH)
    entries = jnp.where(iota(square, 0) == iota(square, 1), taper_ref[...], 0.0)
    table_ref[...] = jnp.broadcast_to(jnp.sum(entries, axis=1, keepdims=True), (REACH, W))
    rinv = jnp.where(lanes_ref[0:1, :] < count_ref[0], invv_ref[...], 0.0)
    column = col_ref[...]
    outer, inner = column // Q, column % Q
    scaled = [jnp.where(outer == a, rinv, 0.0) for a in range(Q)]
    whole = anom_ref[...]
    mean = jnp.sum(whole, axis=0, keepdims=True) * (1.0 / K)
    anom = whole - mean
    left = [anom * scaled[a] for a in range(Q)]
    row = iota((16, slots), 0)
    rows = jnp.where(row < Q, innov_ref[...] * rinv, jnp.where(row < 2 * Q, mean * rinv, 0.0))
    left.append(jnp.where(row % Q == outer, rows, 0.0))
    lhi, llo = halves(jnp.concatenate(left, axis=0))
    rhi, rlo = halves(jnp.concatenate([jnp.where(inner == b, anom, 0.0) for b in range(Q)], axis=0))

    def dot(a, b):
        return lax.dot_general(a, b, (((1,), (1,)), ((), ())), preferred_element_type=F32)

    n = Q * K + 16
    both = dot(jnp.concatenate([lhi, llo], axis=0), rhi)
    sums = both[:n] + (both[n:] + dot(lhi, rlo))
    lane = iota((1, Q * K), 1) // K
    spread = jnp.zeros((8, Q * K), F32)
    product = left[Q][:8] * mean
    for b in range(Q):
        spread = jnp.where(lane == b, jnp.sum(jnp.where(inner == b, product, 0.0), axis=1, keepdims=True), spread)
    factor = jnp.where(iota((8, 1), 0) < Q, 1.0, 0.5)
    vectors = sums[Q * K : Q * K + 8] + spread * factor
    on = iota((K, W), 0) == iota((K, W), 1) % K
    for a in range(Q):
        for i in range(2):
            u = 2 * a + i
            here = sums[K * a : K * (a + 1), W * i : W * (i + 1)]
            sums_ref[K * u : K * (u + 1), :] = here
            sums_ref[GRAM + 2 * U + u : GRAM + 2 * U + u + 1, :] = jnp.sum(jnp.where(on, here, 0.0), axis=0, keepdims=True)
            sums_ref[GRAM + u : GRAM + u + 1, :] = vectors[a : a + 1, W * i : W * (i + 1)]
            sums_ref[GRAM + U + u : GRAM + U + u + 1, :] = vectors[Q + a : Q + a + 1, W * i : W * (i + 1)]
    store(right_ref, mix(sums_ref, table_ref, -1))


def left_kernel(taper_ref, sums_ref, left_ref):
    store(left_ref, mix(sums_ref, taper_ref, 1))


def put(out_ref, parts):
    folded, bvec, mvec, diag = parts
    out_ref[0:HALF, :] = folded
    out_ref[HALF : HALF + 8, :] = bvec
    out_ref[HALF + 8 : HALF + 16, :] = mvec
    out_ref[HALF + 16 : HALF + 24, :] = diag


def get(ref):
    return [ref[0:HALF, :]] + [ref[HALF + 8 * i : HALF + 8 * (i + 1), :] for i in range(3)]


def own_kernel(taper_ref, sums_ref, own_ref):
    put(own_ref, mix(sums_ref, taper_ref, 0))


def before_kernel(own_ref, before_ref, out_ref):
    put(out_ref, [x + y for x, y in zip(get(own_ref), decode(before_ref[...]))])


def after_kernel(own_ref, after_ref, out_ref):
    store(out_ref, [x + y for x, y in zip(get(own_ref), decode(after_ref[...]))])


def members_kernel(ens_ref, mean_ref, anom_ref):
    for c in range(ens_ref.shape[0]):
        members = ens_ref[c].astype(F32)
        mean = jnp.sum(members, axis=0, keepdims=True) * (1.0 / K)
        mean_ref[c : c + 1, :] = mean
        anom_ref[K * c : K * (c + 1), :] = (members - mean).astype(BF16)


def finish_kernel(parts_ref, mean_ref, anom_ref, out_ref, buf, sems):
    width = W
    groups = U
    n = W // K
    lane = iota((1, width), 1) // K
    diagonal = iota((width, width), 0) // K == iota((width, width), 1) // K
    eye = jnp.where(iota((K, width), 0) == iota((K, width), 1) % K, 1.0, 0.0)
    row, col = iota((K, W), 0), iota((K, W), 1) % K
    left_half = iota((K, W), 1) < K

    def spread(x):
        tall = jnp.concatenate([x] * n, axis=0)
        return jnp.where(diagonal, tall, jnp.zeros_like(tall))

    def dot(a, b):
        return jnp.dot(a, b, preferred_element_type=F32)

    def times(left, right):
        count = len(left)
        parts = [halves(x) for x in left]
        hi = [p[0] for p in parts]
        lo = [p[1] for p in parts]
        rhi, rlo = halves(right)
        first = dot(jnp.concatenate(hi + lo, axis=0), spread(rhi))
        second = dot(jnp.concatenate(hi, axis=0), spread(rlo))
        out = first[: count * K] + (first[count * K :] + second)
        return [out[i * K : (i + 1) * K] for i in range(count)]

    def lane_sums(x):
        out = jnp.zeros_like(x)
        for cc in range(n):
            out = jnp.where(lane == cc, jnp.sum(jnp.where(lane == cc, x, 0.0), axis=1, keepdims=True), out)
        return out

    folded, bvec, mvec, diag = decode(parts_ref[0])
    for lag in range(1, parts_ref.shape[0]):
        more = decode(parts_ref[lag])
        folded, bvec, mvec, diag = folded + more[0], bvec + more[1], mvec + more[2], diag + more[3]
    units = [None] * U
    for v in range(U // 2):
        here = folded[K * v : K * (v + 1)]
        if v % 2 == 0:
            square = jnp.transpose(folded[K * v : K * (v + 2)])
            upper, lower = square[:K], square[K:]
            turned = jnp.where(left_half, upper, pltpu.roll(lower, K, 1))
        else:
            turned = jnp.where(left_half, pltpu.roll(upper, K, 1), lower)
        units[v] = jnp.where(row <= col, here, turned)
        units[v + U // 2] = jnp.where(row == col, diag[v : v + 1], jnp.where(row > col, here, turned))
    bvec = [bvec[g : g + 1] for g in range(groups)]
    mvec = [mvec[g : g + 1] for g in range(groups)]
    parts = []
    for g in range(groups):
        line = eye * mvec[g]
        high, low = halves(line)
        parts += [high, low, (line - high.astype(F32) - low.astype(F32)).astype(BF16)]
    ones = jnp.where(diagonal, 1.0, 0.0).astype(BF16)
    across = dot(jnp.concatenate(parts, axis=0), ones)
    across = [sum(across[K * (3 * g + i) : K * (3 * g + i + 1)] for i in range(3)) for g in range(groups)]
    amat = [
        units[g] + mvec[g] + across[g] + (K - 1.0) * eye
        for g in range(groups)
    ]
    norms = jnp.concatenate([jnp.sum(a * a, axis=0, keepdims=True) for a in amat], axis=0)
    scale = jnp.sqrt(lane_sums(norms))
    scale = [scale[g : g + 1] for g in range(groups)]
    square = [times([a], a)[0] for a in amat]
    inverse = [1.0 / s for s in scale]
    one, two, three, four, five = TWO_STEPS
    x1 = [i * a for a, i in zip(amat, inverse)]
    x2 = [(i * i) * q for q, i in zip(square, inverse)]
    more = [times([p, q], q) for p, q in zip(x1, x2)]
    zval = [one * eye + two * p + three * q + (four * m[0] + five * m[1]) for p, q, m in zip(x1, x2, more)]
    more = [times([p, z], z) for p, z in zip(x1, zval)]
    more = [times([z, m[1]], m[0]) for z, m in zip(zval, more)]
    third = [times([m[0], m[1]], m[0]) for m in more]
    last = [times([four * m[1] + five * t[1]], t[0])[0] for m, t in zip(more, third)]
    zval = [one * z + two * m[1] + three * t[1] + y for z, m, t, y in zip(zval, more, third, last)]
    weights = []
    for g in range(groups):
        inner = lane_sums(zval[g] * bvec[g])
        shift = jnp.sum(zval[g] * inner, axis=0, keepdims=True) * inverse[g]
        weights.append((zval[g] * jnp.sqrt((K - 1.0) * inverse[g]) + shift).astype(BF16))
    copies = []
    for g in range(groups):
        mixed = dot(spread(weights[g]), anom_ref[width * g : width * (g + 1), :])
        for cc in range(n):
            c = n * g + cc
            buf[c] = (mean_ref[c : c + 1, :] + mixed[K * cc : K * (cc + 1)]).astype(BF16)
        copies.append(pltpu.make_async_copy(buf.at[pl.ds(n * g, n)], out_ref.at[pl.ds(n * g, n)], sems.at[g]))
        copies[-1].start()
    for copy in copies:
        copy.wait()


def on_device(ensemble, obs_anomaly, innovation, inv_variance, obs_column, obs_count, taper):
    slots = obs_anomaly.shape[1]
    _, ncol, _, points = ensemble.shape
    vmem = pl.BlockSpec(memory_space=VMEM)
    smem = pl.BlockSpec(memory_space=pltpu.SMEM)
    params = pltpu.CompilerParams(vmem_limit_bytes=48 * 2**20)
    sent = jax.ShapeDtypeStruct((SENT, W), BF16)
    kept = jax.ShapeDtypeStruct((HALF + 24, W), F32)

    def cost(flops):
        return pl.CostEstimate(flops=flops, bytes_accessed=2**19, transcendentals=0)

    lanes = pl.pallas_call(
        lanes_kernel,
        out_shape=jax.ShapeDtypeStruct((8, slots), jnp.int32),
        out_specs=vmem,
        compiler_params=params,
        cost_estimate=cost(10**9),
        name="lane_numbers",
    )()
    sums, table, right = pl.pallas_call(
        obs_kernel,
        out_shape=[jax.ShapeDtypeStruct((GRAM + 3 * U, W), F32), jax.ShapeDtypeStruct((REACH, W), F32), sent],
        in_specs=[smem] + [vmem] * 6,
        out_specs=[vmem] * 3,
        compiler_params=params,
        name="obs_sums",
    )(obs_count, taper[None], lanes, obs_anomaly, innovation[None], inv_variance[None], obs_column[None])
    count = lax.axis_size("space")
    before = lax.ppermute(right, "space", [(i, (i + 1) % count) for i in range(count)])
    left = pl.pallas_call(
        left_kernel,
        out_shape=sent,
        in_specs=[vmem, vmem],
        out_specs=vmem,
        compiler_params=params,
        cost_estimate=cost(10**8),
        name="left_sums",
    )(table, sums)
    after = lax.ppermute(left, "space", [((i + 1) % count, i) for i in range(count)])
    own = pl.pallas_call(
        own_kernel,
        out_shape=kept,
        in_specs=[vmem, vmem],
        out_specs=vmem,
        compiler_params=params,
        cost_estimate=cost(10**8),
        name="own_sums",
    )(table, sums)
    mean, anomalies = pl.pallas_call(
        members_kernel,
        out_shape=[jax.ShapeDtypeStruct((ncol, points), F32), jax.ShapeDtypeStruct((ncol * K, points), BF16)],
        in_specs=[vmem],
        out_specs=[vmem, vmem],
        compiler_params=params,
        cost_estimate=cost(10**8),
        name="member_means",
    )(ensemble[0])
    own = pl.pallas_call(
        before_kernel,
        out_shape=kept,
        in_specs=[vmem] * 2,
        out_specs=vmem,
        compiler_params=params,
        name="add_before",
    )(own, before)
    mixed = pl.pallas_call(
        after_kernel,
        out_shape=sent,
        in_specs=[vmem] * 2,
        out_specs=vmem,
        compiler_params=params,
        name="add_after",
    )(own, after)
    parts = lax.all_gather(mixed, "lag")
    out = pl.pallas_call(
        finish_kernel,
        out_shape=jax.ShapeDtypeStruct((ncol, K, points), BF16),
        in_specs=[vmem] * 3,
        out_specs=pl.BlockSpec(memory_space=pl.ANY),
        scratch_shapes=[VMEM((ncol, K, points), BF16), pltpu.SemaphoreType.DMA((U,))],
        compiler_params=params,
        name="transform_apply",
    )(parts, mean, anomalies)
    return out[None]


def solution(mesh):
    placed = (
        P("lag", "space", None, None),
        P(None, ("space", "lag")),
        P(("space", "lag")),
        P(("space", "lag")),
        P(("space", "lag")),
        P(("space", "lag")),
        P(),
    )
    return jax.shard_map(
        on_device,
        mesh=mesh,
        in_specs=placed,
        out_specs=P("lag", "space", None, None),
        check_vma=False,
    )
```

```python
import jax
import jax.numpy as jnp
from jax import lax
from jax.experimental import pallas as pl
from jax.experimental.pallas import tpu as pltpu
from jax.sharding import PartitionSpec as P

TWO_STEPS = (2.25, -2.4375, 1.6875, -0.5625, 0.0625)
K = 64
REACH = 32
U = 8
W = 2 * K
Q = 4
GRAM = U * K
HALF = GRAM // 2
SENT = HALF + 40
F32 = jnp.float32
BF16 = jnp.bfloat16
VMEM = pltpu.VMEM


def halves(x):
    high = x.astype(BF16)
    return high, (x - high.astype(F32)).astype(BF16)


def iota(shape, axis):
    return lax.broadcasted_iota(jnp.int32, shape, axis)


def encode(folded, bvec, mvec, diag):
    bhi, blo = halves(bvec)
    mhi, mlo = halves(mvec)
    rest = [x.astype(F32) for x in (bhi, blo, mhi, mlo)]
    return jnp.concatenate([folded, *rest, diag], axis=0).astype(BF16)


def decode(sent):
    whole = sent.astype(F32)
    bhi, blo, mhi, mlo, diag = (whole[HALF + 8 * i : HALF + 8 * (i + 1)] for i in range(5))
    return whole[:HALF], bhi + blo, mhi + mlo, diag


def mix(sums_ref, taper_ref, side):
    lane = iota((1, W), 1)
    row, col = iota((K, W), 0), iota((K, W), 1) % K

    def at(distance):
        d = min(abs(distance), REACH - 1)
        return taper_ref[d : d + 1, :]

    def same(f):
        return at(2 * f)

    def crossed(f):
        return jnp.where(lane < K, at(2 * f + 1), at(2 * f - 1))

    upper = row <= col
    half = U // 2
    straight, cross = {}, {}
    for f in range(1 - half + U * side, U + U * side):
        straight[f] = jnp.where(upper, same(f), same(f - half))
        cross[f] = jnp.where(upper, crossed(f), crossed(f - half))
    out = [None] * half
    for u in range(U):
        here = sums_ref[K * u : K * (u + 1), :]
        swapped = pltpu.roll(here, K, 1)
        for v in range(half):
            f = u - v + U * side
            term = here * straight[f] + swapped * cross[f]
            out[v] = term if u == 0 else out[v] + term
    folded = jnp.concatenate(out, axis=0)
    sub = iota((U, W), 0)
    vectors = []
    for start in (GRAM, GRAM + U, GRAM + 2 * U):
        here = sums_ref[start : start + U, :]
        swapped = pltpu.roll(here, K, 1)
        total = jnp.zeros((U, W), F32)
        for d in range(U):
            f, g = U * side - d, U * side - d + U
            turned, also = (pltpu.roll(x, d, 0) if d else x for x in (here, swapped))
            total = total + turned * jnp.where(sub >= d, same(f), same(g))
            total = total + also * jnp.where(sub >= d, crossed(f), crossed(g))
        vectors.append(total)
    return folded, vectors[0], vectors[1], jnp.where(sub < half, pltpu.roll(vectors[2], half, 0), 0.0)


def store(out_ref, parts):
    out_ref[...] = encode(*parts)


def lanes_kernel(out_ref):
    out_ref[...] = iota(out_ref.shape, 1)


def obs_kernel(count_ref, taper_ref, lanes_ref, anom_ref, innov_ref, invv_ref, col_ref, sums_ref, table_ref, right_ref):
    slots = anom_ref.shape[1]
    square = (REACH, REACH)
    entries = jnp.where(iota(square, 0) == iota(square, 1), taper_ref[...], 0.0)
    table_ref[...] = jnp.broadcast_to(jnp.sum(entries, axis=1, keepdims=True), (REACH, W))
    rinv = jnp.where(lanes_ref[0:1, :] < count_ref[0], invv_ref[...], 0.0)
    column = col_ref[...]
    outer, inner = column // Q, column % Q
    scaled = [jnp.where(outer == a, rinv, 0.0) for a in range(Q)]
    whole = anom_ref[...]
    mean = jnp.sum(whole, axis=0, keepdims=True) * (1.0 / K)
    anom = whole - mean
    left = [anom * scaled[a] for a in range(Q)]
    row = iota((16, slots), 0)
    rows = jnp.where(row < Q, innov_ref[...] * rinv, jnp.where(row < 2 * Q, mean * rinv, 0.0))
    left.append(jnp.where(row % Q == outer, rows, 0.0))
    lhi, llo = halves(jnp.concatenate(left, axis=0))
    rhi, rlo = halves(jnp.concatenate([jnp.where(inner == b, anom, 0.0) for b in range(Q)], axis=0))

    def dot(a, b):
        return lax.dot_general(a, b, (((1,), (1,)), ((), ())), preferred_element_type=F32)

    n = Q * K + 16
    both = dot(jnp.concatenate([lhi, llo], axis=0), rhi)
    sums = both[:n] + (both[n:] + dot(lhi, rlo))
    lane = iota((1, Q * K), 1) // K
    spread = jnp.zeros((8, Q * K), F32)
    product = left[Q][:8] * mean
    for b in range(Q):
        spread = jnp.where(lane == b, jnp.sum(jnp.where(inner == b, product, 0.0), axis=1, keepdims=True), spread)
    factor = jnp.where(iota((8, 1), 0) < Q, 1.0, 0.5)
    vectors = sums[Q * K : Q * K + 8] + spread * factor
    on = iota((K, W), 0) == iota((K, W), 1) % K
    for a in range(Q):
        for i in range(2):
            u = 2 * a + i
            here = sums[K * a : K * (a + 1), W * i : W * (i + 1)]
            sums_ref[K * u : K * (u + 1), :] = here
            sums_ref[GRAM + 2 * U + u : GRAM + 2 * U + u + 1, :] = jnp.sum(jnp.where(on, here, 0.0), axis=0, keepdims=True)
            sums_ref[GRAM + u : GRAM + u + 1, :] = vectors[a : a + 1, W * i : W * (i + 1)]
            sums_ref[GRAM + U + u : GRAM + U + u + 1, :] = vectors[Q + a : Q + a + 1, W * i : W * (i + 1)]
    store(right_ref, mix(sums_ref, table_ref, -1))


def left_kernel(taper_ref, sums_ref, left_ref):
    store(left_ref, mix(sums_ref, taper_ref, 1))


def put(out_ref, parts):
    folded, bvec, mvec, diag = parts
    out_ref[0:HALF, :] = folded
    out_ref[HALF : HALF + 8, :] = bvec
    out_ref[HALF + 8 : HALF + 16, :] = mvec
    out_ref[HALF + 16 : HALF + 24, :] = diag


def get(ref):
    return [ref[0:HALF, :]] + [ref[HALF + 8 * i : HALF + 8 * (i + 1), :] for i in range(3)]


def own_kernel(taper_ref, sums_ref, own_ref):
    put(own_ref, mix(sums_ref, taper_ref, 0))


def before_kernel(own_ref, before_ref, out_ref):
    put(out_ref, [x + y for x, y in zip(get(own_ref), decode(before_ref[...]))])


def after_kernel(own_ref, after_ref, out_ref):
    store(out_ref, [x + y for x, y in zip(get(own_ref), decode(after_ref[...]))])


def members_kernel(ens_ref, mean_ref, anom_ref):
    for c in range(ens_ref.shape[0]):
        members = ens_ref[c].astype(F32)
        mean = jnp.sum(members, axis=0, keepdims=True) * (1.0 / K)
        mean_ref[c : c + 1, :] = mean
        anom_ref[K * c : K * (c + 1), :] = (members - mean).astype(BF16)


def finish_kernel(parts_ref, mean_ref, anom_ref, out_ref, buf, sems):
    width = W
    groups = U
    n = W // K
    lane = iota((1, width), 1) // K
    diagonal = iota((width, width), 0) // K == iota((width, width), 1) // K
    eye = jnp.where(iota((K, width), 0) == iota((K, width), 1) % K, 1.0, 0.0)
    row, col = iota((K, W), 0), iota((K, W), 1) % K
    left_half = iota((K, W), 1) < K

    def spread(x):
        zero = jnp.zeros_like(x)
        return jnp.concatenate([jnp.where(left_half, x, zero), jnp.where(left_half, zero, x)], axis=0)

    def dot(a, b):
        return jnp.dot(a, b, preferred_element_type=F32)

    def times(left, right):
        count = len(left)
        parts = [halves(x) for x in left]
        hi = [p[0] for p in parts]
        lo = [p[1] for p in parts]
        rhi, rlo = halves(right)
        first = dot(jnp.concatenate(hi + lo, axis=0), spread(rhi))
        second = dot(jnp.concatenate(hi, axis=0), spread(rlo))
        out = first[: count * K] + (first[count * K :] + second)
        return [out[i * K : (i + 1) * K] for i in range(count)]

    def lane_sums(x):
        out = jnp.zeros_like(x)
        for cc in range(n):
            out = jnp.where(lane == cc, jnp.sum(jnp.where(lane == cc, x, 0.0), axis=1, keepdims=True), out)
        return out

    folded, bvec, mvec, diag = decode(parts_ref[0])
    for lag in range(1, parts_ref.shape[0]):
        more = decode(parts_ref[lag])
        folded, bvec, mvec, diag = folded + more[0], bvec + more[1], mvec + more[2], diag + more[3]
    units = [None] * U
    for v in range(U // 2):
        here = folded[K * v : K * (v + 1)]
        if v % 2 == 0:
            square = jnp.transpose(folded[K * v : K * (v + 2)])
            upper, lower = square[:K], square[K:]
            turned = jnp.where(left_half, upper, pltpu.roll(lower, K, 1))
        else:
            turned = jnp.where(left_half, pltpu.roll(upper, K, 1), lower)
        units[v] = jnp.where(row <= col, here, turned)
        units[v + U // 2] = jnp.where(row == col, diag[v : v + 1], jnp.where(row > col, here, turned))
    bvec = [bvec[g : g + 1] for g in range(groups)]
    mvec = [mvec[g : g + 1] for g in range(groups)]
    parts = []
    for g in range(groups):
        line = eye * mvec[g]
        high, low = halves(line)
        parts += [high, low, (line - high.astype(F32) - low.astype(F32)).astype(BF16)]
    ones = jnp.where(diagonal, 1.0, 0.0).astype(BF16)
    across = dot(jnp.concatenate(parts, axis=0), ones)
    across = [sum(across[K * (3 * g + i) : K * (3 * g + i + 1)] for i in range(3)) for g in range(groups)]
    amat = [
        units[g] + mvec[g] + across[g] + (K - 1.0) * eye
        for g in range(groups)
    ]
    norms = jnp.concatenate([jnp.sum(a * a, axis=0, keepdims=True) for a in amat], axis=0)
    scale = jnp.sqrt(lane_sums(norms))
    scale = [scale[g : g + 1] for g in range(groups)]
    square = [times([a], a)[0] for a in amat]
    inverse = [1.0 / s for s in scale]
    one, two, three, four, five = TWO_STEPS
    x1 = [i * a for a, i in zip(amat, inverse)]
    x2 = [(i * i) * q for q, i in zip(square, inverse)]
    more = [times([p, q], q) for p, q in zip(x1, x2)]
    zval = [one * eye + two * p + three * q + (four * m[0] + five * m[1]) for p, q, m in zip(x1, x2, more)]
    more = [times([p, z], z) for p, z in zip(x1, zval)]
    more = [times([z, m[1]], m[0]) for z, m in zip(zval, more)]
    third = [times([m[0], m[1]], m[0]) for m in more]
    last = [times([four * m[1] + five * t[1]], t[0])[0] for m, t in zip(more, third)]
    zval = [one * z + two * m[1] + three * t[1] + y for z, m, t, y in zip(zval, more, third, last)]
    weights = []
    for g in range(groups):
        inner = lane_sums(zval[g] * bvec[g])
        shift = jnp.sum(zval[g] * inner, axis=0, keepdims=True) * inverse[g]
        weights.append((zval[g] * jnp.sqrt((K - 1.0) * inverse[g]) + shift).astype(BF16))
    copies = []
    for g in range(groups):
        mixed = dot(spread(weights[g]), anom_ref[width * g : width * (g + 1), :])
        for cc in range(n):
            c = n * g + cc
            buf[c] = (mean_ref[c : c + 1, :] + mixed[K * cc : K * (cc + 1)]).astype(BF16)
        copies.append(pltpu.make_async_copy(buf.at[pl.ds(n * g, n)], out_ref.at[pl.ds(n * g, n)], sems.at[g]))
        copies[-1].start()
    for copy in copies:
        copy.wait()


def on_device(ensemble, obs_anomaly, innovation, inv_variance, obs_column, obs_count, taper):
    slots = obs_anomaly.shape[1]
    _, ncol, _, points = ensemble.shape
    vmem = pl.BlockSpec(memory_space=VMEM)
    smem = pl.BlockSpec(memory_space=pltpu.SMEM)
    params = pltpu.CompilerParams(vmem_limit_bytes=48 * 2**20)
    sent = jax.ShapeDtypeStruct((SENT, W), BF16)
    kept = jax.ShapeDtypeStruct((HALF + 24, W), F32)

    def cost(flops):
        return pl.CostEstimate(flops=flops, bytes_accessed=2**19, transcendentals=0)

    lanes = pl.pallas_call(
        lanes_kernel,
        out_shape=jax.ShapeDtypeStruct((8, slots), jnp.int32),
        out_specs=vmem,
        compiler_params=params,
        cost_estimate=cost(10**9),
        name="lane_numbers",
    )()
    sums, table, right = pl.pallas_call(
        obs_kernel,
        out_shape=[jax.ShapeDtypeStruct((GRAM + 3 * U, W), F32), jax.ShapeDtypeStruct((REACH, W), F32), sent],
        in_specs=[smem] + [vmem] * 6,
        out_specs=[vmem] * 3,
        compiler_params=params,
        name="obs_sums",
    )(obs_count, taper[None], lanes, obs_anomaly, innovation[None], inv_variance[None], obs_column[None])
    count = lax.axis_size("space")
    before = lax.ppermute(right, "space", [(i, (i + 1) % count) for i in range(count)])
    left = pl.pallas_call(
        left_kernel,
        out_shape=sent,
        in_specs=[vmem, vmem],
        out_specs=vmem,
        compiler_params=params,
        cost_estimate=cost(10**8),
        name="left_sums",
    )(table, sums)
    after = lax.ppermute(left, "space", [((i + 1) % count, i) for i in range(count)])
    own = pl.pallas_call(
        own_kernel,
        out_shape=kept,
        in_specs=[vmem, vmem],
        out_specs=vmem,
        compiler_params=params,
        cost_estimate=cost(10**8),
        name="own_sums",
    )(table, sums)
    mean, anomalies = pl.pallas_call(
        members_kernel,
        out_shape=[jax.ShapeDtypeStruct((ncol, points), F32), jax.ShapeDtypeStruct((ncol * K, points), BF16)],
        in_specs=[vmem],
        out_specs=[vmem, vmem],
        compiler_params=params,
        cost_estimate=cost(10**8),
        name="member_means",
    )(ensemble[0])
    own = pl.pallas_call(
        before_kernel,
        out_shape=kept,
        in_specs=[vmem] * 2,
        out_specs=vmem,
        compiler_params=params,
        name="add_before",
    )(own, before)
    mixed = pl.pallas_call(
        after_kernel,
        out_shape=sent,
        in_specs=[vmem] * 2,
        out_specs=vmem,
        compiler_params=params,
        name="add_after",
    )(own, after)
    parts = lax.all_gather(mixed, "lag")
    out = pl.pallas_call(
        finish_kernel,
        out_shape=jax.ShapeDtypeStruct((ncol, K, points), BF16),
        in_specs=[vmem] * 3,
        out_specs=pl.BlockSpec(memory_space=pl.ANY),
        scratch_shapes=[VMEM((ncol, K, points), BF16), pltpu.SemaphoreType.DMA((U,))],
        compiler_params=params,
        name="transform_apply",
    )(parts, mean, anomalies)
    return out[None]


def solution(mesh):
    placed = (
        P("lag", "space", None, None),
        P(None, ("space", "lag")),
        P(("space", "lag")),
        P(("space", "lag")),
        P(("space", "lag")),
        P(("space", "lag")),
        P(),
    )
    return jax.shard_map(
        on_device,
        mesh=mesh,
        in_specs=placed,
        out_specs=P("lag", "space", None, None),
        check_vma=False,
    )
```
